32 devices in a mesh: dp: 8 (over z, y), tensor: 4 (over x, core).
Axes of the slice: x: 2, y: 2, z: 4, core: 2. Of those that a mesh axis runs over, the one named last changes fastest.
Arguments:
- final_input: bfloat16 [4096, 4096], P('dp'), may hold values from -20 to 20
- norm_gain: bfloat16 [4096], replicated, may hold values from 0.5 to 2
- value_weight: bfloat16 [4096, 1024], P(None, 'tensor'), may hold values from -0.09375 to 0.09375
- out_weight: bfloat16 [4096, 4096], P('tensor'), may hold values from -0.1875 to 0.1875
- cluster: int32 [4096, 1], P('dp'), may hold values from 0 to 31; in each aligned block of 512 rows (0 to 511, 512 to 1023, ...) at most 32 rows name the same one
- priority: int32 [4096], P('dp'), may hold values from 0 to 4095, each once
Outputs:
- best_match: float32 [4096], P('dp')
The draws below stay inside these ranges and needn't reach their ends.
Inputs may be any that keep to these rules, and one draw needn't show every extreme that they name: Among the rows of one device (aligned blocks of 512 documents), no cluster holds more than 32 documents, and some cluster holds exactly 32. `priority`: every rank appears exactly once.
All inputs are finite; a program needn't handle non-finite values.
Results may differ from the reference program's by a relative error of at most 0.0012.
Values may be sent and summed in bfloat16 or wider, within the bound.
A program may use at most 128 MiB of HBM per device.

```python
import math
import jax
import jax.numpy as jnp
import numpy as np
from jax import lax

D = 4096
HEADS = 32
KV_HEADS = 8
HEAD_DIM = 128
DOC_DEV = 512
DOCS = 4096
CLUSTERS = 32
BUCKET = 32
N_DP = 8
N_TENSOR = 4


def draw_final_input(key, part):
    key = jax.random.fold_in(key, 7)
    keys = jax.random.split(key, 6)
    chosen = jax.random.randint(keys[0], (DOCS,), 0, 16)
    strength = jnp.exp(jax.random.uniform(keys[1], (DOCS, 1), jnp.float32, math.log(0.5), math.log(2.0)))
    row_scale = jnp.exp(jax.random.uniform(keys[2], (DOCS, 1), jnp.float32, math.log(0.3), math.log(3.0)))
    column_rough = jnp.exp(jax.random.uniform(keys[3], (1, D), jnp.float32, math.log(0.7), math.log(1.4)))
    position = jnp.arange(D, dtype=jnp.float32)[None, :] / D
    templates = jax.random.normal(keys[4], (16, D), jnp.float32)
    noise_part = jax.random.normal(keys[5], (DOCS, D), jnp.float32)
    column_ramp = 1.0 + 2.0 * position
    combined = strength * templates[chosen] + noise_part
    return jnp.clip(row_scale * column_ramp * column_rough * combined, -20.0, 20.0).astype(jnp.bfloat16)


def shard_levels(key, extent, pieces, low, top_value):
    gain = 1.0
    for dim, parts in pieces:
        heights = jax.random.uniform(jax.random.fold_in(jax.random.fold_in(key, 6), dim), (parts,), jnp.float32, low / len(pieces), top_value / len(pieces))
        gain = gain * jnp.repeat(jnp.exp(heights), extent[dim] // parts).reshape((-1,) + (1,) * (len(extent) - 1 - dim))
    return gain


def deal_out(rng, own, number, rows, count, top, limit, slope):
    order = jax.random.permutation(rng, count)
    packed, usual = load_shares(count, rows * top, limit, slope, True), load_shares(count, rows * top, limit, slope, False)
    places = jnp.arange(count)

    def named(lengths, turn):
        used = int((lengths > 0).sum())
        fixed = max(1, used // 4)
        passed = fixed + (places - fixed + turn * (used - fixed)) % max(1, count - fixed)
        return jnp.zeros((count,), jnp.int32).at[order[jnp.where(places < fixed, places, passed)]].set(jnp.asarray(lengths, jnp.int32))

    lengths = jnp.where(number % 4 == 0, named(packed, number // 4), named(usual, number - number // 4 - 1))
    mixed = jax.random.permutation(jax.random.fold_in(own, 3), count)
    giver, sink = mixed[0:count // 2 * 2:2], mixed[1:count // 2 * 2:2]
    room = jnp.minimum(lengths[giver] - 1, limit - lengths[sink]) // 2
    room = jnp.where((giver == order[0]) | (sink == order[0]) | (lengths[sink] == 0), 0, jnp.maximum(room, 0))
    passed = jax.random.randint(jax.random.fold_in(own, 4), (count // 2,), 0, 1 << 20) % (room + 1)
    lengths = lengths.at[giver].add(-passed).at[sink].add(passed)
    items = jnp.searchsorted(jnp.cumsum(lengths), jnp.arange(rows * top), side="right").astype(jnp.int32)
    listing = items.reshape(top, rows).T
    listing = listing[jax.random.permutation(jax.random.fold_in(own, 1), rows)]
    turn = jax.random.randint(jax.random.fold_in(own, 2), (rows, 1), 0, top)
    return jnp.take_along_axis(listing, (jnp.arange(top)[None, :] + turn) % top, axis=1)


def load_shares(count, total, bound, skew, full):
    loads = [(1 << 20) // math.isqrt(standing ** skew) + 1 for standing in range(1, count + 1)]
    largest = bound if full else min(bound, max(-(-total // count), total * loads[0] // sum(loads)))
    least = 1 if total - largest >= count - 1 else 0
    given, spare = [largest] + [least] * (count - 1), total - largest - least * (count - 1)
    while spare > 0:
        movable = [i for i in range(1, count) if given[i] < largest] or [i for i in range(1, count) if given[i] < bound]
        mass, budget = sum([loads[i] for i in movable]), spare
        for i in movable:
            extra = min(bound - given[i], max(1, budget * loads[i] // mass), spare)
            given[i] = given[i] + extra
            spare = spare - extra
    return np.array(given)


def scatter_about(key, shape, spread, limit, cuts=(), held_as=jnp.bfloat16):
    array = jax.random.normal(key, shape, jnp.float32) * spread
    if len(cuts) > 0:
        array = shard_levels(key, shape, cuts, -0.22, 0.18) * array
    return jnp.clip(array, min=-limit, max=limit).astype(held_as)


def setup_inputs(seed: int = 0) -> dict:
    seeds = jax.random.split(jax.random.key(seed), 7)
    final_input = draw_final_input(jax.random.fold_in(seeds[6], 71), 0)
    norm_gain = jnp.clip(jnp.exp(jax.random.uniform(seeds[1], (D,), jnp.float32, math.log(0.5), math.log(2.0))), 0.5, 2.0).astype(jnp.bfloat16)
    value_weight = scatter_about(seeds[2], (D, KV_HEADS * HEAD_DIM), D ** -0.5, 0.09375, ((1, 4),))
    out_weight = scatter_about(seeds[3], (HEADS * HEAD_DIM, D), (KV_HEADS * HEAD_DIM) ** -0.5, 0.1875, ((0, 4),))
    cluster_keys = jax.random.split(jax.random.fold_in(seeds[4], 1), DOCS // DOC_DEV)
    cluster_turns = jax.random.permutation(jax.random.fold_in(seeds[4], 3), DOCS // DOC_DEV)
    cluster = jax.vmap(lambda own, number: deal_out(jax.random.fold_in(seeds[4], 2), own, number, DOC_DEV, CLUSTERS, 1, BUCKET, 2))(cluster_keys, cluster_turns).reshape((DOCS, 1))
    priority = jax.random.permutation(seeds[5], DOCS).astype(jnp.int32)
    return {"final_input": final_input, "norm_gain": norm_gain, "value_weight": value_weight, "out_weight": out_weight, "cluster": cluster, "priority": priority}


def reference(final_input, norm_gain, value_weight, out_weight, cluster, priority):
    inputs_f32 = final_input.astype(jnp.float32)
    scaling = lax.rsqrt(lax.optimization_barrier(jnp.mean(inputs_f32 * inputs_f32, axis=1, keepdims=True)) + 1e-05)
    normed = (inputs_f32 * scaling * norm_gain.astype(jnp.float32)).astype(jnp.bfloat16)
    values = jnp.dot(normed, value_weight, preferred_element_type=jnp.float32).astype(jnp.bfloat16)
    group_size = HEADS // KV_HEADS
    attended = jnp.broadcast_to(values.reshape(DOCS, KV_HEADS, 1, HEAD_DIM), (DOCS, KV_HEADS, group_size, HEAD_DIM)).reshape(DOCS, HEADS * HEAD_DIM)
    block_width = HEADS * HEAD_DIM // N_TENSOR
    attention = jnp.zeros((DOCS, D), jnp.float32)
    for part_index in range(N_TENSOR):
        lower = part_index * block_width
        upper = lower + block_width
        term_block = jnp.dot(attended[:, lower:upper], out_weight[lower:upper], preferred_element_type=jnp.float32).astype(jnp.bfloat16)
        attention = attention + lax.optimization_barrier(term_block).astype(jnp.float32)
    hidden = inputs_f32 + attention
    squares = lax.optimization_barrier(jnp.sum(hidden * hidden, axis=1))
    embedded = hidden * lax.rsqrt(squares + 1e-06)[:, None]
    cluster_ids = cluster[:, 0].astype(jnp.int32)
    order = jnp.argsort(cluster_ids, stable=True).astype(jnp.int32)
    sorted_ids = cluster_ids[order]
    starts = jnp.searchsorted(sorted_ids, jnp.arange(CLUSTERS, dtype=jnp.int32)).astype(jnp.int32)
    within = jnp.arange(DOCS, dtype=jnp.int32) - starts[sorted_ids]
    capacity = N_DP * BUCKET
    table = jnp.full((CLUSTERS, capacity), -1, jnp.int32).at[sorted_ids, within].set(order)

    def one_cluster(members):
        present = members >= 0
        safe_index = jnp.where(present, members, 0)
        vectors = embedded[safe_index]
        ranking = jnp.where(present, priority[safe_index], DOCS)
        products = jnp.dot(vectors, vectors.T, precision=lax.Precision.HIGHEST, preferred_element_type=jnp.float32)
        allowed = (ranking[None, :] < ranking[:, None]) & present[None, :]
        highest = lax.optimization_barrier(jnp.max(jnp.where(allowed, products, -2.0), axis=1))
        return jnp.maximum(highest, -1.0)
    results = lax.map(one_cluster, table, batch_size=8)
    target = jnp.where(table >= 0, table, DOCS)
    return jnp.zeros((DOCS,), jnp.float32).at[target.reshape(-1)].set(results.reshape(-1), mode='drop')
```

```python
import functools

import jax
import jax.numpy as jnp
from jax import lax
from jax.experimental import pallas as pl
from jax.experimental.pallas import tpu as pltpu
from jax.sharding import PartitionSpec as P

HEADS = 32
KV_HEADS = 8
HEAD_DIM = 128
CLU_DEV = 4
CHUNKS = 4
MESH = pl.DeviceIdType.MESH
BF16 = jnp.bfloat16
F32 = jnp.float32
I32 = jnp.int32


def iota(shape, dim):
    return lax.broadcasted_iota(I32, shape, dim)


def kernel(
    owners, bucket,
    x_hbm, gain_ref, vw_hbm, ow_hbm, cluster_ref, priority_ref, out_ref,
    x_v, vw_v, ow_v, values, send_a, keep_a, recv_a, send_b, recv_b,
    place, send_c, recv_c, send_r, recv_r, gram, recv_e, send_f, recv_f, best_t, send_h, recv_h,
    in_sem, a_s, a_r, b_s, b_r, c_s, c_r, r_s, r_r, e_s, e_r, f_s, f_r, g_s, g_r, h_s, h_r,
):
    rows, width = x_v.shape
    chunk = recv_b.shape[2]
    chunks = recv_b.shape[0]
    part = chunk * chunks
    per_owner = CLU_DEV * bucket
    capacity = owners * bucket
    sentinel = owners * rows
    me = lax.axis_index("dp")
    t = lax.axis_index("tensor")
    xh, core = t // 2, t % 2
    partner = 2 * xh + (1 - core)
    across = 2 * (1 - xh) + core
    half = rows // 2

    def load_x(i):
        span = pl.ds(i * half, half)
        return pltpu.make_async_copy(x_hbm.at[span], x_v.at[span], in_sem.at[i])

    load_vw = pltpu.make_async_copy(vw_hbm, vw_v, in_sem.at[2])
    load_ow = pltpu.make_async_copy(ow_hbm, ow_v, in_sem.at[3])
    load_x(0).start()
    load_vw.start()
    load_x(1).start()
    load_ow.start()

    barrier = pltpu.get_barrier_semaphore()

    def greet(o, _):
        pl.semaphore_signal(barrier, inc=1, device_id=(lax.rem(me + o, owners), t), device_id_type=MESH)
        return 0

    for o in range(1, 4):
        pl.semaphore_signal(barrier, inc=1, device_id=(me, lax.rem(t + o, 4)), device_id_type=MESH)
    lax.fori_loop(1, owners, greet, 0)

    def project(i, _):
        span = pl.ds(pl.multiple_of(i * half, half), half)
        xs = x_v[span, :].astype(F32)
        scaling = lax.rsqrt(jnp.sum(xs * xs, axis=1, keepdims=True) * (1.0 / width) + 1e-05)
        normed = (xs * scaling * gain_ref[...].astype(F32)).astype(BF16)
        values[span, :] = jnp.dot(normed, vw_v[...], preferred_element_type=F32).astype(BF16)
        return 0

    load_x(0).wait()
    load_x(1).wait()
    load_vw.wait()
    lax.fori_loop(0, 2, project, 0)
    load_ow.wait()

    def copy_a(k):
        return pltpu.make_async_remote_copy(
            send_a.at[k], recv_a.at[k], a_s.at[k], a_r.at[k], device_id=(me, partner), device_id_type=MESH)

    def copy_b(k):
        return pltpu.make_async_remote_copy(
            send_b.at[k], recv_b.at[k], b_s.at[k], b_r.at[k], device_id=(me, across), device_id_type=MESH)

    def copy_c(k, to, frm):
        return pltpu.make_async_remote_copy(
            send_c.at[k, to], recv_c.at[k, frm], c_s.at[k, to], c_r.at[k, frm],
            device_id=(to, t), device_id_type=MESH)

    def copy_r(to, frm):
        return pltpu.make_async_remote_copy(
            send_r.at[to], recv_r.at[frm], r_s.at[to], r_r.at[frm], device_id=(to, t), device_id_type=MESH)

    def copy_h(to, frm):
        return pltpu.make_async_remote_copy(
            send_h, recv_h.at[frm], h_s.at[to], h_r.at[frm], device_id=(to, t), device_id_type=MESH)

    def term(quarter, k):
        columns = pl.ds(pl.multiple_of(quarter * part + k * chunk, chunk), chunk)
        w = ow_v[:, columns].astype(F32)
        kv_local = values.shape[1] // HEAD_DIM
        w = w.reshape(kv_local, HEADS // KV_HEADS, HEAD_DIM, chunk)
        w = jnp.sum(w, axis=1).reshape(kv_local * HEAD_DIM, chunk).astype(BF16)
        return jnp.dot(values[...], w, preferred_element_type=F32).astype(BF16)

    def stage_a(k, _):
        for h in range(2):
            send_a[k, h] = term(2 * h + 1 - core, k)

        @pl.when(k == 0)
        def _():
            pl.semaphore_wait(barrier, 3 + owners - 1)

        copy_a(k).start()
        for h in range(2):
            keep_a[k, h] = term(2 * h + core, k)

        @pl.when(k > 0)
        def _():
            stage_b(k - 1)

        return 0

    def stage_b(k):
        copy_a(k).wait_recv()
        send_b[k] = (keep_a[k, 1 - xh].astype(F32) + recv_a[k, 1 - xh].astype(F32)).astype(BF16)
        copy_b(k).start()

    lax.fori_loop(0, chunks, stage_a, 0)
    stage_b(chunks - 1)

    cluster_col = cluster_ref[...]
    square = (rows, rows)
    i0, i1 = iota(square, 0), iota(square, 1)
    cluster_row = jnp.sum(jnp.where(i0 == i1, cluster_col, 0), axis=0, keepdims=True)
    slot_row = jnp.sum(
        jnp.where((cluster_col == cluster_row) & (i0 < i1), 1, 0), axis=0, keepdims=True)
    flat_row = cluster_row * bucket + slot_row
    place[...] = jnp.where(iota(place.shape, 0) == flat_row, 1.0, 0.0).astype(BF16)

    rank = priority_ref[...]
    high, low = (rank // 128).astype(F32), (rank % 128).astype(F32)
    line = iota((8, rows), 0)
    meta = jnp.where(line == 0, high, jnp.where(line == 1, low, jnp.where(line == 2, 1.0, 0.0)))
    meta = meta.astype(BF16)

    def rank_block(to, _):
        s = iota((128, rows), 0)
        hit = (s + to * per_owner == flat_row) & (s < per_owner)
        got = lax.dot_general(
            meta, jnp.where(hit, 1.0, 0.0).astype(BF16), (((1,), (1,)), ((), ())),
            preferred_element_type=F32)
        line = got[0:1] * 128.0 + got[1:2] + (1.0 - got[2:3]) * float(sentinel)
        send_r[to] = jnp.broadcast_to(line, (8, 128))
        return 0

    lax.fori_loop(0, owners, rank_block, 0)
    recv_r[me] = send_r[me]

    def start_r(o, _):
        copy_r(lax.rem(me + o, owners), me).start()
        return 0

    lax.fori_loop(1, owners, start_r, 0)

    def stage_c(k, _):
        copy_b(k).wait_recv()
        columns = pl.ds(pl.multiple_of(t * part + k * chunk, chunk), chunk)
        attention = keep_a[k, xh].astype(F32) + recv_a[k, xh].astype(F32) + recv_b[k].astype(F32)
        hidden = (x_v[:, columns].astype(F32) + attention).astype(BF16)
        placed = jnp.dot(place[...], hidden, preferred_element_type=F32).astype(BF16)
        send_c[k] = placed.reshape(owners, per_owner, chunk)

        def start_c(o, _):
            copy_c(k, lax.rem(me + o, owners), me).start()
            return 0

        lax.fori_loop(1, owners, start_c, 0)
        recv_c[k, me] = send_c[k, me]
        return 0

    lax.fori_loop(0, chunks, stage_c, 0)

    gram[...] = jnp.zeros_like(gram)

    def stage_d(k, _):
        def wait_c(o, _):
            copy_c(k, me, lax.rem(me + o, owners)).wait_recv()
            return 0

        lax.fori_loop(1, owners, wait_c, 0)
        for c in range(CLU_DEV):
            if bucket % 16 == 0:
                members = recv_c[k, :, c * bucket:(c + 1) * bucket, :].reshape(capacity, chunk)
            else:
                every = recv_c[k].reshape(owners * per_owner, chunk)
                shape = (capacity, owners * per_owner)
                r = iota(shape, 0)
                pick = (r // bucket) * per_owner + c * bucket + r % bucket == iota(shape, 1)
                members = jnp.dot(
                    jnp.where(pick, 1.0, 0.0).astype(BF16), every, preferred_element_type=F32).astype(BF16)
            gram[c] += lax.dot_general(
                members, members, (((1,), (1,)), ((), ())), preferred_element_type=F32)
        return 0

    lax.fori_loop(0, chunks, stage_d, 0)

    def copy_e(h):
        return pltpu.make_async_remote_copy(
            gram.at[2 * h + 1 - core], recv_e.at[h], e_s.at[h], e_r.at[h],
            device_id=(me, partner), device_id_type=MESH)

    copy_f = pltpu.make_async_remote_copy(
        send_f, recv_f, f_s, f_r, device_id=(me, across), device_id_type=MESH)
    copy_e(1 - xh).start()
    copy_e(xh).start()

    def wait_r(o, _):
        copy_r(me, lax.rem(me + o, owners)).wait_recv()
        return 0

    lax.fori_loop(1, owners, wait_r, 0)
    ranks = recv_r[:, 0, :]
    r = iota((capacity, owners), 0)
    expand = jnp.where(r // bucket == iota((capacity, owners), 1), 1.0, 0.0)
    spread = jnp.dot(expand, ranks, precision=lax.Precision.HIGHEST, preferred_element_type=F32)
    r = iota((capacity, 128), 0)
    rank_col = jnp.sum(
        jnp.where(iota((capacity, 128), 1) == t * bucket + r % bucket, spread, 0.0), axis=1, keepdims=True)
    eye = iota((capacity, capacity), 0) == iota((capacity, capacity), 1)
    rank_row = jnp.sum(jnp.where(eye, rank_col, 0.0), axis=0, keepdims=True)

    copy_e(1 - xh).wait_recv()
    send_f[...] = gram[2 * (1 - xh) + core] + recv_e[1 - xh]
    copy_f.start()
    copy_e(xh).wait_recv()
    mine = gram[2 * xh + core] + recv_e[xh]
    copy_f.wait_recv()
    total = mine + recv_f[...]
    diagonal = jnp.where(eye, total, 0.0)
    norm_row = lax.rsqrt(jnp.sum(diagonal, axis=0, keepdims=True) + 1e-06)
    norm_col = lax.rsqrt(jnp.sum(diagonal, axis=1, keepdims=True) + 1e-06)
    similarity = total * norm_col * norm_row
    highest = jnp.max(jnp.where(rank_col < rank_row, similarity, -2.0), axis=0, keepdims=True)
    highest = jnp.maximum(highest, -1.0)
    best_t[t] = jnp.broadcast_to(highest, (8, capacity))

    def copy_g(to, frm):
        return pltpu.make_async_remote_copy(
            best_t.at[frm], best_t.at[frm], g_s.at[to], g_r.at[frm], device_id=(me, to), device_id_type=MESH)

    for o in range(1, 4):
        copy_g(lax.rem(t + o, 4), t).start()
    for o in range(1, 4):
        copy_g(t, lax.rem(t + o, 4)).wait_recv()
    line = iota((8, capacity), 0)
    rows_h = jnp.zeros((8, capacity), F32)
    for c in range(CLU_DEV):
        rows_h = jnp.where(line == c, best_t[c], rows_h)
    send_h[...] = rows_h

    def start_h(o, _):
        copy_h(lax.rem(me + o, owners), me).start()
        return 0

    lax.fori_loop(1, owners, start_h, 0)
    recv_h[me] = rows_h

    def wait_h(o, _):
        copy_h(me, lax.rem(me + o, owners)).wait_recv()
        return 0

    pick = jnp.where(iota((capacity, rows), 0) == me * bucket + slot_row, 1.0, 0.0)
    lax.fori_loop(1, owners, wait_h, 0)
    returned = recv_h[...].reshape(owners * 8, capacity)
    found = jnp.dot(returned, pick, precision=lax.Precision.HIGHEST, preferred_element_type=F32)
    where = (cluster_row // CLU_DEV) * 8 + cluster_row % CLU_DEV
    out_ref[...] = jnp.sum(
        jnp.where(iota((owners * 8, rows), 0) == where, found, 0.0), axis=0, keepdims=True)

    def sent_k(k, _):
        copy_a(k).wait_send()
        copy_b(k).wait_send()

        def sent_c(o, _):
            copy_c(k, lax.rem(me + o, owners), me).wait_send()
            return 0

        lax.fori_loop(1, owners, sent_c, 0)
        return 0

    lax.fori_loop(0, chunks, sent_k, 0)

    def sent(o, _):
        to = lax.rem(me + o, owners)
        copy_r(to, me).wait_send()
        copy_h(to, me).wait_send()
        return 0

    lax.fori_loop(1, owners, sent, 0)
    copy_e(1 - xh).wait_send()
    copy_e(xh).wait_send()
    copy_f.wait_send()
    for o in range(1, 4):
        copy_g(lax.rem(t + o, 4), t).wait_send()


def shards(final_input, norm_gain, value_weight, out_weight, cluster, priority):
    rows, width = final_input.shape
    owners = lax.axis_size("dp")
    tensor = lax.axis_size("tensor")
    part = width // tensor
    chunk = part // CHUNKS
    bucket = max(2, 2 * rows // (CLU_DEV * owners))
    per_owner = CLU_DEV * bucket
    capacity = owners * bucket
    kv = value_weight.shape[1]
    vmem = pl.BlockSpec(memory_space=pltpu.VMEM)
    anywhere = pl.BlockSpec(memory_space=pl.ANY)
    dma = pltpu.SemaphoreType.DMA
    best = pl.pallas_call(
        functools.partial(kernel, owners, bucket),
        out_shape=jax.ShapeDtypeStruct((1, rows), F32),
        in_specs=[anywhere, vmem, anywhere, anywhere, vmem, vmem],
        out_specs=vmem,
        scratch_shapes=[
            pltpu.VMEM((rows, width), BF16),
            pltpu.VMEM((width, kv), BF16),
            pltpu.VMEM(out_weight.shape, BF16),
            pltpu.VMEM((rows, kv), BF16),
            pltpu.VMEM((CHUNKS, 2, rows, chunk), BF16),
            pltpu.VMEM((CHUNKS, 2, rows, chunk), BF16),
            pltpu.VMEM((CHUNKS, 2, rows, chunk), BF16),
            pltpu.VMEM((CHUNKS, rows, chunk), BF16),
            pltpu.VMEM((CHUNKS, rows, chunk), BF16),
            pltpu.VMEM((owners * per_owner, rows), BF16),
            pltpu.VMEM((CHUNKS, owners, per_owner, chunk), BF16),
            pltpu.VMEM((CHUNKS, owners, per_owner, chunk), BF16),
            pltpu.VMEM((owners, 8, 128), F32),
            pltpu.VMEM((owners, 8, 128), F32),
            pltpu.VMEM((CLU_DEV, capacity, capacity), F32),
            pltpu.VMEM((2, capacity, capacity), F32),
            pltpu.VMEM((capacity, capacity), F32),
            pltpu.VMEM((capacity, capacity), F32),
            pltpu.VMEM((CLU_DEV, 8, capacity), F32),
            pltpu.VMEM((8, capacity), F32),
            pltpu.VMEM((owners, 8, capacity), F32),
            dma((4,)),
            dma((CHUNKS,)), dma((CHUNKS,)),
            dma((CHUNKS,)), dma((CHUNKS,)),
            dma((CHUNKS, owners)), dma((CHUNKS, owners)),
            dma((owners,)), dma((owners,)),
            dma((2,)), dma((2,)),
            dma, dma,
            dma((4,)), dma((4,)),
            dma((owners,)), dma((owners,)),
        ],
        compiler_params=pltpu.CompilerParams(
            collective_id=0, has_side_effects=True, vmem_limit_bytes=56 * 1024 * 1024),
        cost_estimate=pl.CostEstimate(flops=6_000_000_000, bytes_accessed=16_000_000, transcendentals=0),
    )(final_input, norm_gain.reshape(1, width), value_weight, out_weight, cluster, priority.reshape(1, rows))
    return best.reshape(rows)


def solution(mesh):
    in_specs = (P("dp", None), P(), P(None, "tensor"), P("tensor", None), P("dp", None), P("dp"))
    out_specs = P("dp")
    return jax.shard_map(shards, mesh=mesh, in_specs=in_specs, out_specs=out_specs, check_vma=False)
```

```python
import functools

import jax
import jax.numpy as jnp
from jax import lax
from jax.experimental import pallas as pl
from jax.experimental.pallas import tpu as pltpu
from jax.sharding import PartitionSpec as P

HEADS = 32
KV_HEADS = 8
HEAD_DIM = 128
CLU_DEV = 4
CHUNKS = 8
LAG = 5
MESH = pl.DeviceIdType.MESH
BF16 = jnp.bfloat16
F32 = jnp.float32
I32 = jnp.int32


def iota(shape, dim):
    return lax.broadcasted_iota(I32, shape, dim)


def drain(ref, sem):
    pltpu.make_async_copy(ref, ref, sem).wait()


def kernel(
    owners, bucket,
    x_hbm, gain_ref, vw_hbm, ow_hbm, cluster_ref, priority_ref, out_ref,
    x_v, vw_v, ow_v, values, send_a, keep_a, recv_a, send_b, recv_b,
    place, send_c, recv_c, send_r, recv_r, gram, recv_e, send_f, recv_f, best_t, send_h, recv_h,
    in_sem, a_s, a_r, b_s, b_r, c_s, c_r, r_s, r_r, e_s, e_r, f_s, f_r, g_s, g_r, h_s, h_r,
):
    rows, width = x_v.shape
    chunks, _, chunk = recv_b.shape
    part = chunk * chunks
    side = recv_c.shape[3]
    per_owner = 2 * side
    capacity = owners * bucket
    sentinel = owners * rows
    me = lax.axis_index("dp")
    t = lax.axis_index("tensor")
    xh, core = t // 2, t % 2
    partner = 2 * xh + (1 - core)
    across = 2 * (1 - xh) + core
    half = rows // 2

    def peer(o):
        found, bit = 0, 1
        while bit < owners:
            found = found + lax.rem(me // bit + o // bit, 2) * bit
            bit = 2 * bit
        return found

    def each_peer(act):
        def step(i, _):
            act(peer(owners - 1 - i))
            return 0

        lax.fori_loop(0, owners - 1, step, 0)

    def load_x(i):
        span = pl.ds(i * half, half)
        return pltpu.make_async_copy(x_hbm.at[span], x_v.at[span], in_sem.at[i])

    load_vw = pltpu.make_async_copy(vw_hbm, vw_v, in_sem.at[2])
    load_ow = pltpu.make_async_copy(ow_hbm, ow_v, in_sem.at[3])
    load_x(0).start()
    load_vw.start()
    load_x(1).start()
    load_ow.start()

    barrier = pltpu.get_barrier_semaphore()
    for o in range(1, 4):
        pl.semaphore_signal(barrier, inc=1, device_id=(me, lax.rem(t + o, 4)), device_id_type=MESH)
    each_peer(lambda to: pl.semaphore_signal(barrier, inc=1, device_id=(to, t), device_id_type=MESH))

    cluster_row = cluster_ref[...]
    square = (rows, rows)
    i0, i1 = iota(square, 0), iota(square, 1)
    cluster_col = jnp.sum(jnp.where(i0 == i1, cluster_row, 0), axis=1, keepdims=True)
    slot_row = jnp.sum(
        jnp.where((cluster_col == cluster_row) & (i0 < i1), 1, 0), axis=0, keepdims=True)
    flat_row = (cluster_row // 2) * side + (cluster_row % 2) * bucket + slot_row
    place[...] = jnp.where(iota(place.shape, 0) == flat_row, 1.0, 0.0).astype(BF16)

    rank = priority_ref[...]
    high, low = (rank // 128).astype(F32), (rank % 128).astype(F32)
    line = iota((8, rows), 0)
    meta = jnp.where(line == 0, high, jnp.where(line == 1, low, jnp.where(line == 2, 1.0, 0.0)))
    meta = meta.astype(BF16)

    def rank_block(to, _):
        s = iota((128, rows), 0)
        hit = (s + to * per_owner == flat_row) & (s < per_owner)
        got = lax.dot_general(
            meta, jnp.where(hit, 1.0, 0.0).astype(BF16), (((1,), (1,)), ((), ())),
            preferred_element_type=F32)
        line = got[0:1] * 128.0 + got[1:2] + (1.0 - got[2:3]) * float(sentinel)
        send_r[to] = jnp.broadcast_to(line, (8, 128))
        return 0

    lax.fori_loop(0, owners, rank_block, 0)
    recv_r[me] = send_r[me]

    def project(i):
        span = pl.ds(i * half, half)
        xs = x_v[span, :]
        wide = xs.astype(F32)
        scaling = lax.rsqrt(jnp.sum(wide * wide, axis=1, keepdims=True) * (1.0 / width) + 1e-05)
        gained = xs * gain_ref[...].reshape(1, width)
        product = jnp.dot(gained, vw_v[...], preferred_element_type=F32)
        values[span, :] = (product * scaling).astype(BF16)

    load_x(0).wait()
    load_vw.wait()
    project(0)
    load_x(1).wait()
    project(1)
    load_ow.wait()
    pl.semaphore_wait(barrier, 3 + owners - 1)

    def copy_a(k):
        return pltpu.make_async_remote_copy(
            send_a.at[k], recv_a.at[k], a_s.at[k], a_r.at[k], device_id=(me, partner), device_id_type=MESH)

    def copy_b(k):
        return pltpu.make_async_remote_copy(
            send_b.at[k], recv_b.at[k], b_s.at[k], b_r.at[k], device_id=(me, across), device_id_type=MESH)

    def start_c(k, h):
        each_peer(lambda to: pltpu.make_async_remote_copy(
            send_c.at[k, to, h], recv_c.at[k, h, me], c_s.at[k, h], c_r.at[k, h],
            device_id=(to, t), device_id_type=MESH).start())
        recv_c[k, h, me] = send_c[k, me, h]

    def term(quarter, k):
        columns = pl.ds(pl.multiple_of(quarter * part + k * chunk, chunk), chunk)
        w = ow_v[:, columns].astype(F32)
        kv_local = values.shape[1] // HEAD_DIM
        w = w.reshape(kv_local, HEADS // KV_HEADS, HEAD_DIM, chunk)
        w = jnp.sum(w, axis=1).reshape(kv_local * HEAD_DIM, chunk).astype(BF16)
        return jnp.dot(values[...], w, preferred_element_type=F32).astype(BF16)

    def stage_a(k):
        for h in range(2):
            send_a[k, h] = term(2 * h + 1 - core, k)
        copy_a(k).start()
        for h in range(2):
            keep_a[k, h] = term(2 * h + core, k)

    def stage_b(k):
        copy_a(k).wait_recv()
        send_b[k] = (keep_a[k, 1 - xh].astype(F32) + recv_a[k, 1 - xh].astype(F32)).astype(BF16)
        copy_b(k).start()

    def stage_c(k):
        copy_b(k).wait_recv()
        columns = pl.ds(pl.multiple_of(t * part + k * chunk, chunk), chunk)
        attention = keep_a[k, xh].astype(F32) + recv_a[k, xh].astype(F32) + recv_b[k].astype(F32)
        hidden = (x_v[:, columns].astype(F32) + attention).astype(BF16)
        placed = jnp.dot(place[...], hidden, preferred_element_type=F32).astype(BF16)
        send_c[k] = placed.reshape(owners, 2, side, chunk)
        start_c(k, 1 - xh)

        @pl.when(k % 2 == 1)
        def _():
            start_c(k // 2, xh)

    def step(s, _):
        @pl.when(s < chunks)
        def _():
            stage_a(s)

        @pl.when((s > 0) & (s <= chunks))
        def _():
            stage_b(s - 1)

        @pl.when(s >= LAG)
        def _():
            stage_c(s - LAG)

        return 0

    lax.fori_loop(0, chunks + LAG, step, 0)
    lax.fori_loop(chunks // 2, chunks, lambda k, _: start_c(k, xh) or 0, 0)
    each_peer(lambda to: pltpu.make_async_remote_copy(
        send_r.at[to], recv_r.at[me], r_s, r_r, device_id=(to, t), device_id_type=MESH).start())

    others = pl.ds(0, owners - 1)
    gram[...] = jnp.zeros_like(gram)

    def stage_d(h):
        def one(k, _):
            drain(recv_c.at[k, h, others], c_r.at[k, h])
            for c in range(2):
                if bucket % 16 == 0:
                    members = recv_c[k, h, :, c * bucket:(c + 1) * bucket, :].reshape(capacity, chunk)
                else:
                    every = recv_c[k, h].reshape(owners * side, chunk)
                    shape = (capacity, owners * side)
                    r = iota(shape, 0)
                    pick = (r // bucket) * side + c * bucket + r % bucket == iota(shape, 1)
                    members = jnp.dot(
                        jnp.where(pick, 1.0, 0.0).astype(BF16), every, preferred_element_type=F32)
                    members = members.astype(BF16)
                gram[2 * h + c] += lax.dot_general(
                    members, members, (((1,), (1,)), ((), ())), preferred_element_type=F32)
            return 0

        lax.fori_loop(0, chunks, one, 0)

    def copy_e(h):
        return pltpu.make_async_remote_copy(
            gram.at[2 * h + 1 - core], recv_e.at[h], e_s.at[h], e_r.at[h],
            device_id=(me, partner), device_id_type=MESH)

    copy_f = pltpu.make_async_remote_copy(
        send_f, recv_f, f_s, f_r, device_id=(me, across), device_id_type=MESH)

    stage_d(1 - xh)
    copy_e(1 - xh).start()
    copy_e(1 - xh).wait_recv()
    send_f[...] = gram[2 * (1 - xh) + core] + recv_e[1 - xh]
    copy_f.start()

    drain(recv_r.at[others], r_r)
    ranks = recv_r[:, 0, :]
    r = iota((capacity, owners), 0)
    expand = jnp.where(r // bucket == iota((capacity, owners), 1), 1.0, 0.0)
    spread = jnp.dot(expand, ranks, precision=lax.Precision.HIGHEST, preferred_element_type=F32)
    r = iota((capacity, 128), 0)
    lane = xh * side + core * bucket + r % bucket
    rank_col = jnp.sum(
        jnp.where(iota((capacity, 128), 1) == lane, spread, 0.0), axis=1, keepdims=True)
    eye = iota((capacity, capacity), 0) == iota((capacity, capacity), 1)
    rank_row = jnp.sum(jnp.where(eye, rank_col, 0.0), axis=0, keepdims=True)
    pick = jnp.where(iota((capacity, rows), 0) == me * bucket + slot_row, 1.0, 0.0)

    stage_d(xh)
    copy_e(xh).start()
    copy_f.wait_recv()
    copy_e(xh).wait_recv()
    total = gram[2 * xh + core] + recv_e[xh] + recv_f[...]
    diagonal = jnp.where(eye, total, 0.0)
    norm_row = lax.rsqrt(jnp.sum(diagonal, axis=0, keepdims=True) + 1e-06)
    norm_col = lax.rsqrt(jnp.sum(diagonal, axis=1, keepdims=True) + 1e-06)
    similarity = total * norm_col * norm_row
    highest = jnp.max(jnp.where(rank_col < rank_row, similarity, -2.0), axis=0, keepdims=True)
    highest = jnp.maximum(highest, -1.0)
    best_t[t] = jnp.broadcast_to(highest, (8, capacity))

    def copy_g(to, frm):
        return pltpu.make_async_remote_copy(
            best_t.at[frm], best_t.at[frm], g_s.at[to], g_r.at[frm], device_id=(me, to), device_id_type=MESH)

    for o in range(1, 4):
        copy_g(lax.rem(t + o, 4), t).start()
    for o in range(1, 4):
        copy_g(t, lax.rem(t + o, 4)).wait_recv()
    line = iota((8, capacity), 0)
    rows_h = jnp.zeros((8, capacity), F32)
    for c in range(CLU_DEV):
        rows_h = jnp.where(line == c, best_t[c], rows_h)
    send_h[...] = rows_h
    each_peer(lambda to: pltpu.make_async_remote_copy(
        send_h, recv_h.at[me], h_s, h_r, device_id=(to, t), device_id_type=MESH).start())
    recv_h[me] = rows_h
    drain(recv_h.at[others], h_r)
    returned = recv_h[...].reshape(owners * 8, capacity)
    found = jnp.dot(returned, pick, precision=lax.Precision.HIGHEST, preferred_element_type=F32)
    where = (cluster_row // CLU_DEV) * 8 + cluster_row % CLU_DEV
    out_ref[...] = jnp.sum(
        jnp.where(iota((owners * 8, rows), 0) == where, found, 0.0), axis=0, keepdims=True)

    def sent_k(k, _):
        copy_a(k).wait_send()
        copy_b(k).wait_send()
        for h in range(2):
            drain(recv_c.at[k, h, others], c_s.at[k, h])
        return 0

    lax.fori_loop(0, chunks, sent_k, 0)
    drain(recv_r.at[others], r_s)
    drain(recv_h.at[others], h_s)
    copy_e(1 - xh).wait_send()
    copy_e(xh).wait_send()
    copy_f.wait_send()
    for o in range(1, 4):
        copy_g(lax.rem(t + o, 4), t).wait_send()


def shards(final_input, norm_gain, value_weight, out_weight, cluster, priority):
    rows, width = final_input.shape
    owners = lax.axis_size("dp")
    tensor = lax.axis_size("tensor")
    part = width // tensor
    chunk = part // CHUNKS
    bucket = max(2, 2 * rows // (CLU_DEV * owners))
    side = max(16, 2 * bucket)
    per_owner = 2 * side
    capacity = owners * bucket
    kv = value_weight.shape[1]
    vmem = pl.BlockSpec(memory_space=pltpu.VMEM)
    anywhere = pl.BlockSpec(memory_space=pl.ANY)
    dma = pltpu.SemaphoreType.DMA
    best = pl.pallas_call(
        functools.partial(kernel, owners, bucket),
        out_shape=jax.ShapeDtypeStruct((1, rows), F32),
        in_specs=[anywhere, vmem, anywhere, anywhere, vmem, vmem],
        out_specs=vmem,
        scratch_shapes=[
            pltpu.VMEM((rows, width), BF16),
            pltpu.VMEM((width, kv), BF16),
            pltpu.VMEM(out_weight.shape, BF16),
            pltpu.VMEM((rows, kv), BF16),
            pltpu.VMEM((CHUNKS, 2, rows, chunk), BF16),
            pltpu.VMEM((CHUNKS, 2, rows, chunk), BF16),
            pltpu.VMEM((CHUNKS, 2, rows, chunk), BF16),
            pltpu.VMEM((CHUNKS, rows, chunk), BF16),
            pltpu.VMEM((CHUNKS, rows, chunk), BF16),
            pltpu.VMEM((owners * per_owner, rows), BF16),
            pltpu.VMEM((CHUNKS, owners, 2, side, chunk), BF16),
            pltpu.VMEM((CHUNKS, 2, owners, side, chunk), BF16),
            pltpu.VMEM((owners, 8, 128), F32),
            pltpu.VMEM((owners, 8, 128), F32),
            pltpu.VMEM((CLU_DEV, capacity, capacity), F32),
            pltpu.VMEM((2, capacity, capacity), F32),
            pltpu.VMEM((capacity, capacity), F32),
            pltpu.VMEM((capacity, capacity), F32),
            pltpu.VMEM((CLU_DEV, 8, capacity), F32),
            pltpu.VMEM((8, capacity), F32),
            pltpu.VMEM((owners, 8, capacity), F32),
            dma((4,)),
            dma((CHUNKS,)), dma((CHUNKS,)),
            dma((CHUNKS,)), dma((CHUNKS,)),
            dma((CHUNKS, 2)), dma((CHUNKS, 2)),
            dma, dma,
            dma((2,)), dma((2,)),
            dma, dma,
            dma((4,)), dma((4,)),
            dma, dma,
        ],
        compiler_params=pltpu.CompilerParams(
            collective_id=0, has_side_effects=True, vmem_limit_bytes=56 * 1024 * 1024),
        cost_estimate=pl.CostEstimate(flops=6_000_000_000, bytes_accessed=16_000_000, transcendentals=0),
    )(final_input, norm_gain, value_weight, out_weight, cluster.reshape(1, rows), priority.reshape(1, rows))
    return best.reshape(rows)


def solution(mesh):
    in_specs = (P("dp", None), P(), P(None, "tensor"), P("tensor", None), P("dp", None), P("dp"))
    out_specs = P("dp")
    return jax.shard_map(shards, mesh=mesh, in_specs=in_specs, out_specs=out_specs, check_vma=False)
```

```python
import functools

import jax
import jax.numpy as jnp
from jax import lax
from jax.experimental import pallas as pl
from jax.experimental.pallas import tpu as pltpu
from jax.sharding import PartitionSpec as P

HEADS = 32
KV_HEADS = 8
HEAD_DIM = 128
CLU_DEV = 4
CHUNKS = 8
LAG = 5
MESH = pl.DeviceIdType.MESH
BF16 = jnp.bfloat16
F32 = jnp.float32
I32 = jnp.int32


def iota(shape, dim):
    return lax.broadcasted_iota(I32, shape, dim)


def drain(ref, sem):
    pltpu.make_async_copy(ref, ref, sem).wait()


def kernel(
    owners, bucket,
    x_hbm, gain_ref, vw_hbm, ow_hbm, cluster_ref, priority_ref, out_ref,
    x_v, vw_v, ow_v, scale_v, values, send_a, keep_a, recv_a, send_b, recv_b,
    place, send_c, recv_c, send_r, recv_r, gram, recv_e, send_f, recv_f, best_t, send_h, recv_h,
    in_sem, a_s, a_r, b_s, b_r, c_s, c_r, r_s, r_r, e_s, e_r, f_s, f_r, g_s, g_r, h_s, h_r,
):
    rows, width = x_v.shape
    chunks, _, chunk = recv_b.shape
    part = chunk * chunks
    side = recv_c.shape[3]
    per_owner = 2 * side
    capacity = owners * bucket
    sentinel = owners * rows
    me = lax.axis_index("dp")
    t = lax.axis_index("tensor")
    xh, core = t // 2, t % 2
    partner = 2 * xh + (1 - core)
    across = 2 * (1 - xh) + core
    half = rows // 2

    def peer(o):
        found, bit = 0, 1
        while bit < owners:
            found = found + lax.rem(me // bit + o // bit, 2) * bit
            bit = 2 * bit
        return found

    def each_peer(act):
        def step(i, _):
            act(peer(owners - 1 - i))
            return 0

        lax.fori_loop(0, owners - 1, step, 0)

    def load_x(i):
        span = pl.ds(i * half, half)
        return pltpu.make_async_copy(x_hbm.at[span], x_v.at[span], in_sem.at[i])

    load_vw = pltpu.make_async_copy(vw_hbm, vw_v, in_sem.at[2])
    load_ow = pltpu.make_async_copy(ow_hbm, ow_v, in_sem.at[3])
    load_x(0).start()
    load_vw.start()
    load_x(1).start()

    barrier = pltpu.get_barrier_semaphore()
    for o in range(1, 4):
        pl.semaphore_signal(barrier, inc=1, device_id=(me, lax.rem(t + o, 4)), device_id_type=MESH)
    each_peer(lambda to: pl.semaphore_signal(barrier, inc=1, device_id=(to, t), device_id_type=MESH))

    cluster_row = cluster_ref[...]
    square = (rows, rows)
    i0, i1 = iota(square, 0), iota(square, 1)
    cluster_col = jnp.sum(jnp.where(i0 == i1, cluster_row, 0), axis=1, keepdims=True)
    slot_row = jnp.sum(
        jnp.where((cluster_col == cluster_row) & (i0 < i1), 1, 0), axis=0, keepdims=True)
    flat_row = (cluster_row // 2) * side + (cluster_row % 2) * bucket + slot_row
    place[...] = jnp.where(iota(place.shape, 0) == flat_row, 1.0, 0.0).astype(BF16)

    def project(i):
        span = pl.ds(i * half, half)
        xs = x_v[span, :]
        gained = xs * gain_ref[...].reshape(1, width)
        values[span, :] = jnp.dot(gained, vw_v[...], preferred_element_type=F32).astype(BF16)

    load_x(0).wait()
    load_vw.wait()
    load_ow.start()
    project(0)
    load_x(1).wait()
    project(1)
    load_ow.wait()
    pl.semaphore_wait(barrier, 3 + owners - 1)

    def copy_a(k):
        return pltpu.make_async_remote_copy(
            send_a.at[k], recv_a.at[k], a_s.at[k], a_r.at[k], device_id=(me, partner), device_id_type=MESH)

    def copy_b(k):
        return pltpu.make_async_remote_copy(
            send_b.at[k], recv_b.at[k], b_s.at[k], b_r.at[k], device_id=(me, across), device_id_type=MESH)

    def start_c(k, h):
        each_peer(lambda to: pltpu.make_async_remote_copy(
            send_c.at[k, to, h], recv_c.at[k, h, me], c_s.at[k, h], c_r.at[k, h],
            device_id=(to, t), device_id_type=MESH).start())
        recv_c[k, h, me] = send_c[k, me, h]

    def term(quarter, k):
        columns = pl.ds(pl.multiple_of(quarter * part + k * chunk, chunk), chunk)
        w = ow_v[:, columns].astype(F32)
        kv_local = values.shape[1] // HEAD_DIM
        w = w.reshape(kv_local, HEADS // KV_HEADS, HEAD_DIM, chunk)
        w = jnp.sum(w, axis=1).reshape(kv_local * HEAD_DIM, chunk).astype(BF16)
        return jnp.dot(values[...], w, preferred_element_type=F32).astype(BF16)

    def stage_a(k):
        for h in range(2):
            send_a[k, h] = term(2 * h + 1 - core, k)
        copy_a(k).start()
        for h in range(2):
            keep_a[k, h] = term(2 * h + core, k)

    def stage_b(k):
        copy_a(k).wait_recv()
        send_b[k] = (keep_a[k, 1 - xh].astype(F32) + recv_a[k, 1 - xh].astype(F32)).astype(BF16)
        copy_b(k).start()

    def stage_c(k):
        copy_b(k).wait_recv()
        columns = pl.ds(pl.multiple_of(t * part + k * chunk, chunk), chunk)
        attention = keep_a[k, xh].astype(F32) + recv_a[k, xh].astype(F32) + recv_b[k].astype(F32)
        hidden = (x_v[:, columns].astype(F32) + attention * scale_v[...]).astype(BF16)
        placed = jnp.dot(place[...], hidden, preferred_element_type=F32).astype(BF16)
        send_c[k] = placed.reshape(owners, 2, side, chunk)
        start_c(k, 1 - xh)

        @pl.when(k % 2 == 1)
        def _():
            start_c(k // 2, xh)

    def step(s, _):
        @pl.when(s < chunks)
        def _():
            stage_a(s)

        @pl.when((s > 0) & (s <= chunks))
        def _():
            stage_b(s - 1)

        @pl.when(s >= LAG)
        def _():
            stage_c(s - LAG)

        return 0

    lax.fori_loop(0, 2, step, 0)

    def row_scale(i, _):
        span = pl.ds(pl.multiple_of(i * 128, 128), 128)
        xs = x_v[span, :].astype(F32)
        scale_v[span, :] = lax.rsqrt(jnp.sum(xs * xs, axis=1, keepdims=True) * (1.0 / width) + 1e-05)
        return 0

    lax.fori_loop(0, rows // 128, row_scale, 0)
    lax.fori_loop(2, chunks + LAG, step, 0)
    lax.fori_loop(chunks // 2, chunks, lambda k, _: start_c(k, xh) or 0, 0)
    rank = priority_ref[...]
    high, low = (rank // 128).astype(F32), (rank % 128).astype(F32)
    line = iota((8, rows), 0)
    meta = jnp.where(line == 0, high, jnp.where(line == 1, low, jnp.where(line == 2, 1.0, 0.0)))
    meta = meta.astype(BF16)

    def rank_block(to, _):
        s = iota((128, rows), 0)
        hit = (s + to * per_owner == flat_row) & (s < per_owner)
        got = lax.dot_general(
            meta, jnp.where(hit, 1.0, 0.0).astype(BF16), (((1,), (1,)), ((), ())),
            preferred_element_type=F32)
        line = got[0:1] * 128.0 + got[1:2] + (1.0 - got[2:3]) * float(sentinel)
        send_r[to] = jnp.broadcast_to(line, (8, 128))
        return 0

    lax.fori_loop(0, owners, rank_block, 0)
    recv_r[me] = send_r[me]
    each_peer(lambda to: pltpu.make_async_remote_copy(
        send_r.at[to], recv_r.at[me], r_s, r_r, device_id=(to, t), device_id_type=MESH).start())

    others = pl.ds(0, owners - 1)
    gram[...] = jnp.zeros_like(gram)

    def stage_d(h):
        def one(k, _):
            drain(recv_c.at[k, h, others], c_r.at[k, h])
            for c in range(2):
                if bucket % 16 == 0:
                    members = recv_c[k, h, :, c * bucket:(c + 1) * bucket, :].reshape(capacity, chunk)
                else:
                    every = recv_c[k, h].reshape(owners * side, chunk)
                    shape = (capacity, owners * side)
                    r = iota(shape, 0)
                    pick = (r // bucket) * side + c * bucket + r % bucket == iota(shape, 1)
                    members = jnp.dot(
                        jnp.where(pick, 1.0, 0.0).astype(BF16), every, preferred_element_type=F32)
                    members = members.astype(BF16)
                gram[2 * h + c] += lax.dot_general(
                    members, members, (((1,), (1,)), ((), ())), preferred_element_type=F32)
            return 0

        lax.fori_loop(0, chunks, one, 0)

    def copy_e(h):
        return pltpu.make_async_remote_copy(
            gram.at[2 * h + 1 - core], recv_e.at[h], e_s.at[h], e_r.at[h],
            device_id=(me, partner), device_id_type=MESH)

    copy_f = pltpu.make_async_remote_copy(
        send_f, recv_f, f_s, f_r, device_id=(me, across), device_id_type=MESH)

    stage_d(1 - xh)
    copy_e(1 - xh).start()
    copy_e(1 - xh).wait_recv()
    send_f[...] = gram[2 * (1 - xh) + core] + recv_e[1 - xh]
    copy_f.start()

    drain(recv_r.at[others], r_r)
    ranks = recv_r[:, 0, :]
    r = iota((capacity, owners), 0)
    expand = jnp.where(r // bucket == iota((capacity, owners), 1), 1.0, 0.0)
    spread = jnp.dot(expand, ranks, precision=lax.Precision.HIGHEST, preferred_element_type=F32)
    r = iota((capacity, 128), 0)
    lane = xh * side + core * bucket + r % bucket
    rank_col = jnp.sum(
        jnp.where(iota((capacity, 128), 1) == lane, spread, 0.0), axis=1, keepdims=True)
    eye = iota((capacity, capacity), 0) == iota((capacity, capacity), 1)
    rank_row = jnp.sum(jnp.where(eye, rank_col, 0.0), axis=0, keepdims=True)
    spot = me * bucket + slot_row
    pick = jnp.where(iota((128, rows), 0) == spot % 128, 1.0, 0.0)

    stage_d(xh)
    copy_e(xh).start()
    copy_f.wait_recv()
    copy_e(xh).wait_recv()
    total = gram[2 * xh + core] + recv_e[xh] + recv_f[...]
    diagonal = jnp.where(eye, total, 0.0)
    norm_row = lax.rsqrt(jnp.sum(diagonal, axis=0, keepdims=True) + 1e-06)
    norm_col = lax.rsqrt(jnp.sum(diagonal, axis=1, keepdims=True) + 1e-06)
    similarity = total * norm_col * norm_row
    highest = jnp.max(jnp.where(rank_col < rank_row, similarity, -2.0), axis=0, keepdims=True)
    highest = jnp.maximum(highest, -1.0)
    best_t[t] = jnp.broadcast_to(highest, (8, capacity))

    def copy_g(to, frm):
        return pltpu.make_async_remote_copy(
            best_t.at[frm], best_t.at[frm], g_s.at[to], g_r.at[frm], device_id=(me, to), device_id_type=MESH)

    for o in range(1, 4):
        copy_g(lax.rem(t + o, 4), t).start()
    for o in range(1, 4):
        copy_g(t, lax.rem(t + o, 4)).wait_recv()
    line = iota((8, 128), 0)
    rows_h = jnp.zeros((8, 128), F32)
    for c in range(CLU_DEV):
        for j in range(2):
            rows_h = jnp.where(line == j * CLU_DEV + c, best_t[c, :, j * 128:(j + 1) * 128], rows_h)
    send_h[...] = rows_h
    each_peer(lambda to: pltpu.make_async_remote_copy(
        send_h, recv_h.at[me], h_s, h_r, device_id=(to, t), device_id_type=MESH).start())
    recv_h[me] = rows_h
    drain(recv_h.at[others], h_r)
    returned = recv_h[...].reshape(owners * 8, 128)
    found = jnp.dot(returned, pick, precision=lax.Precision.HIGHEST, preferred_element_type=F32)
    where = (cluster_row // CLU_DEV) * 8 + (spot // 128) * CLU_DEV + cluster_row % CLU_DEV
    out_ref[...] = jnp.sum(
        jnp.where(iota((owners * 8, rows), 0) == where, found, 0.0), axis=0, keepdims=True)

    def sent_k(k, _):
        copy_a(k).wait_send()
        copy_b(k).wait_send()
        for h in range(2):
            drain(recv_c.at[k, h, others], c_s.at[k, h])
        return 0

    lax.fori_loop(0, chunks, sent_k, 0)
    drain(recv_r.at[others], r_s)
    drain(recv_h.at[others], h_s)
    copy_e(1 - xh).wait_send()
    copy_e(xh).wait_send()
    copy_f.wait_send()
    for o in range(1, 4):
        copy_g(lax.rem(t + o, 4), t).wait_send()


def shards(final_input, norm_gain, value_weight, out_weight, cluster, priority):
    rows, width = final_input.shape
    owners = lax.axis_size("dp")
    tensor = lax.axis_size("tensor")
    part = width // tensor
    chunk = part // CHUNKS
    bucket = max(2, 2 * rows // (CLU_DEV * owners))
    side = max(16, 2 * bucket)
    per_owner = 2 * side
    capacity = owners * bucket
    kv = value_weight.shape[1]
    vmem = pl.BlockSpec(memory_space=pltpu.VMEM)
    anywhere = pl.BlockSpec(memory_space=pl.ANY)
    dma = pltpu.SemaphoreType.DMA
    best = pl.pallas_call(
        functools.partial(kernel, owners, bucket),
        out_shape=jax.ShapeDtypeStruct((1, rows), F32),
        in_specs=[anywhere, vmem, anywhere, anywhere, vmem, vmem],
        out_specs=vmem,
        scratch_shapes=[
            pltpu.VMEM((rows, width), BF16),
            pltpu.VMEM((width, kv), BF16),
            pltpu.VMEM(out_weight.shape, BF16),
            pltpu.VMEM((rows, 1), F32),
            pltpu.VMEM((rows, kv), BF16),
            pltpu.VMEM((CHUNKS, 2, rows, chunk), BF16),
            pltpu.VMEM((CHUNKS, 2, rows, chunk), BF16),
            pltpu.VMEM((CHUNKS, 2, rows, chunk), BF16),
            pltpu.VMEM((CHUNKS, rows, chunk), BF16),
            pltpu.VMEM((CHUNKS, rows, chunk), BF16),
            pltpu.VMEM((owners * per_owner, rows), BF16),
            pltpu.VMEM((CHUNKS, owners, 2, side, chunk), BF16),
            pltpu.VMEM((CHUNKS, 2, owners, side, chunk), BF16),
            pltpu.VMEM((owners, 8, 128), F32),
            pltpu.VMEM((owners, 8, 128), F32),
            pltpu.VMEM((CLU_DEV, capacity, capacity), F32),
            pltpu.VMEM((2, capacity, capacity), F32),
            pltpu.VMEM((capacity, capacity), F32),
            pltpu.VMEM((capacity, capacity), F32),
            pltpu.VMEM((CLU_DEV, 8, capacity), F32),
            pltpu.VMEM((8, 128), F32),
            pltpu.VMEM((owners, 8, 128), F32),
            dma((4,)),
            dma((CHUNKS,)), dma((CHUNKS,)),
            dma((CHUNKS,)), dma((CHUNKS,)),
            dma((CHUNKS, 2)), dma((CHUNKS, 2)),
            dma, dma,
            dma((2,)), dma((2,)),
            dma, dma,
            dma((4,)), dma((4,)),
            dma, dma,
        ],
        compiler_params=pltpu.CompilerParams(
            collective_id=0, has_side_effects=True, vmem_limit_bytes=56 * 1024 * 1024),
        cost_estimate=pl.CostEstimate(flops=6_000_000_000, bytes_accessed=16_000_000, transcendentals=0),
    )(final_input, norm_gain, value_weight, out_weight, cluster.reshape(1, rows), priority.reshape(1, rows))
    return best.reshape(rows)


def solution(mesh):
    in_specs = (P("dp", None), P(), P(None, "tensor"), P("tensor", None), P("dp", None), P("dp"))
    out_specs = P("dp")
    return jax.shard_map(shards, mesh=mesh, in_specs=in_specs, out_specs=out_specs, check_vma=False)
```

```python
import functools

import jax
import jax.numpy as jnp
from jax import lax
from jax.experimental import pallas as pl
from jax.experimental.pallas import tpu as pltpu
from jax.sharding import PartitionSpec as P

HEADS = 32
KV_HEADS = 8
HEAD_DIM = 128
CLU_DEV = 4
CHUNKS = 4
LAG = 3
MESH = pl.DeviceIdType.MESH
BF16 = jnp.bfloat16
F32 = jnp.float32
I32 = jnp.int32


def iota(shape, dim):
    return lax.broadcasted_iota(I32, shape, dim)


def drain(ref, sem):
    pltpu.make_async_copy(ref, ref, sem).wait()


def kernel(
    owners, bucket,
    x_hbm, gain_ref, vw_hbm, ow_hbm, cluster_ref, priority_ref, out_ref,
    x_v, vw_v, ow_v, scale_v, values, send_a, keep_a, recv_a, send_b, recv_b,
    place, send_c, recv_c, send_r, recv_r, gram, recv_e, send_f, recv_f, best_t, send_h, recv_h,
    in_sem, a_s, a_r, b_s, b_r, c_s, c_r, r_s, r_r, e_s, e_r, f_s, f_r, g_s, g_r, h_s, h_r,
):
    rows, width = x_v.shape
    chunks, _, chunk = recv_b.shape
    part = chunk * chunks
    side = recv_c.shape[3]
    per_owner = 2 * side
    capacity = owners * bucket
    sentinel = owners * rows
    me = lax.axis_index("dp")
    t = lax.axis_index("tensor")
    xh, core = t // 2, t % 2
    partner = 2 * xh + (1 - core)
    across = 2 * (1 - xh) + core
    half = rows // 2

    def peer(o):
        found, bit = 0, 1
        while bit < owners:
            found = found + lax.rem(me // bit + o // bit, 2) * bit
            bit = 2 * bit
        return found

    def each_peer(act):
        def step(i, _):
            act(peer(owners - 1 - i))
            return 0

        lax.fori_loop(0, owners - 1, step, 0)

    def load_x(i):
        span = pl.ds(i * half, half)
        return pltpu.make_async_copy(x_hbm.at[span], x_v.at[span], in_sem.at[i])

    load_vw = pltpu.make_async_copy(vw_hbm, vw_v, in_sem.at[2])
    load_ow = pltpu.make_async_copy(ow_hbm, ow_v, in_sem.at[3])
    load_x(0).start()
    load_vw.start()
    load_x(1).start()

    barrier = pltpu.get_barrier_semaphore()
    for o in range(1, 4):
        pl.semaphore_signal(barrier, inc=1, device_id=(me, lax.rem(t + o, 4)), device_id_type=MESH)
    each_peer(lambda to: pl.semaphore_signal(barrier, inc=1, device_id=(to, t), device_id_type=MESH))

    cluster_row = cluster_ref[...]
    square = (rows, rows)
    i0, i1 = iota(square, 0), iota(square, 1)
    cluster_col = jnp.sum(jnp.where(i0 == i1, cluster_row, 0), axis=1, keepdims=True)
    slot_row = jnp.sum(
        jnp.where((cluster_col == cluster_row) & (i0 < i1), 1, 0), axis=0, keepdims=True)
    flat_row = (cluster_row // 2) * side + (cluster_row % 2) * bucket + slot_row
    place[...] = jnp.where(iota(place.shape, 0) == flat_row, 1.0, 0.0).astype(BF16)

    def project(i):
        span = pl.ds(i * half, half)
        xs = x_v[span, :]
        gained = xs * gain_ref[...].reshape(1, width)
        values[span, :] = jnp.dot(gained, vw_v[...], preferred_element_type=F32).astype(BF16)

    load_x(0).wait()
    load_vw.wait()
    load_ow.start()
    project(0)
    load_x(1).wait()
    project(1)
    load_ow.wait()
    pl.semaphore_wait(barrier, 3 + owners - 1)

    def copy_a(k):
        return pltpu.make_async_remote_copy(
            send_a.at[k], recv_a.at[k], a_s.at[k], a_r.at[k], device_id=(me, partner), device_id_type=MESH)

    def copy_b(k):
        return pltpu.make_async_remote_copy(
            send_b.at[k], recv_b.at[k], b_s.at[k], b_r.at[k], device_id=(me, across), device_id_type=MESH)

    def start_c(k, h):
        each_peer(lambda to: pltpu.make_async_remote_copy(
            send_c.at[k, to, h], recv_c.at[k, h, me], c_s.at[k, h], c_r.at[k, h],
            device_id=(to, t), device_id_type=MESH).start())
        recv_c[k, h, me] = send_c[k, me, h]

    def term(quarter, k):
        columns = pl.ds(pl.multiple_of(quarter * part + k * chunk, chunk), chunk)
        w = ow_v[:, columns].astype(F32)
        kv_local = values.shape[1] // HEAD_DIM
        w = w.reshape(kv_local, HEADS // KV_HEADS, HEAD_DIM, chunk)
        w = jnp.sum(w, axis=1).reshape(kv_local * HEAD_DIM, chunk).astype(BF16)
        return jnp.dot(values[...], w, preferred_element_type=F32).astype(BF16)

    def stage_a(k):
        for h in range(2):
            send_a[k, h] = term(2 * h + 1 - core, k)
        copy_a(k).start()
        for h in range(2):
            keep_a[k, h] = term(2 * h + core, k)

    def stage_b(k):
        copy_a(k).wait_recv()
        send_b[k] = (keep_a[k, 1 - xh].astype(F32) + recv_a[k, 1 - xh].astype(F32)).astype(BF16)
        copy_b(k).start()

    def stage_c(k):
        copy_b(k).wait_recv()
        columns = pl.ds(pl.multiple_of(t * part + k * chunk, chunk), chunk)
        attention = keep_a[k, xh].astype(F32) + recv_a[k, xh].astype(F32) + recv_b[k].astype(F32)
        hidden = (x_v[:, columns].astype(F32) + attention * scale_v[...]).astype(BF16)
        placed = jnp.dot(place[...], hidden, preferred_element_type=F32).astype(BF16)
        send_c[k] = placed.reshape(owners, 2, side, chunk)
        start_c(k, 1 - xh)

        @pl.when(k % 2 == 1)
        def _():
            start_c(k // 2, xh)

    def step(s, _):
        @pl.when(s < chunks)
        def _():
            stage_a(s)

        @pl.when((s > 0) & (s <= chunks))
        def _():
            stage_b(s - 1)

        @pl.when(s >= LAG)
        def _():
            stage_c(s - LAG)

        return 0

    lax.fori_loop(0, 2, step, 0)

    def row_scale(i, _):
        span = pl.ds(pl.multiple_of(i * 128, 128), 128)
        xs = x_v[span, :].astype(F32)
        scale_v[span, :] = lax.rsqrt(jnp.sum(xs * xs, axis=1, keepdims=True) * (1.0 / width) + 1e-05)
        return 0

    lax.fori_loop(0, rows // 128, row_scale, 0)
    rank = priority_ref[...]
    high, low = (rank // 128).astype(F32), (rank % 128).astype(F32)
    line = iota((8, rows), 0)
    meta = jnp.where(line == 0, high, jnp.where(line == 1, low, jnp.where(line == 2, 1.0, 0.0)))
    meta = meta.astype(BF16)

    def rank_block(to, _):
        s = iota((128, rows), 0)
        hit = (s + to * per_owner == flat_row) & (s < per_owner)
        got = lax.dot_general(
            meta, jnp.where(hit, 1.0, 0.0).astype(BF16), (((1,), (1,)), ((), ())),
            preferred_element_type=F32)
        line = got[0:1] * 128.0 + got[1:2] + (1.0 - got[2:3]) * float(sentinel)
        send_r[to] = jnp.broadcast_to(line, (8, 128))
        return 0

    lax.fori_loop(0, owners, rank_block, 0)
    recv_r[me] = send_r[me]
    each_peer(lambda to: pltpu.make_async_remote_copy(
        send_r.at[to], recv_r.at[me], r_s, r_r, device_id=(to, t), device_id_type=MESH).start())

    lax.fori_loop(2, chunks + LAG, step, 0)
    lax.fori_loop(chunks // 2, chunks, lambda k, _: start_c(k, xh) or 0, 0)
    others = pl.ds(0, owners - 1)
    gram[...] = jnp.zeros_like(gram)

    def stage_d(h):
        def one(k, _):
            drain(recv_c.at[k, h, others], c_r.at[k, h])
            for c in range(2):
                if bucket % 16 == 0:
                    members = recv_c[k, h, :, c * bucket:(c + 1) * bucket, :].reshape(capacity, chunk)
                else:
                    every = recv_c[k, h].reshape(owners * side, chunk)
                    shape = (capacity, owners * side)
                    r = iota(shape, 0)
                    pick = (r // bucket) * side + c * bucket + r % bucket == iota(shape, 1)
                    members = jnp.dot(
                        jnp.where(pick, 1.0, 0.0).astype(BF16), every, preferred_element_type=F32)
                    members = members.astype(BF16)
                gram[2 * h + c] += lax.dot_general(
                    members, members, (((1,), (1,)), ((), ())), preferred_element_type=F32)
            return 0

        lax.fori_loop(0, chunks, one, 0)

    def copy_e(h):
        return pltpu.make_async_remote_copy(
            gram.at[2 * h + 1 - core], recv_e.at[h], e_s.at[h], e_r.at[h],
            device_id=(me, partner), device_id_type=MESH)

    copy_f = pltpu.make_async_remote_copy(
        send_f, recv_f, f_s, f_r, device_id=(me, across), device_id_type=MESH)

    stage_d(1 - xh)
    copy_e(1 - xh).start()
    copy_e(1 - xh).wait_recv()
    send_f[...] = gram[2 * (1 - xh) + core] + recv_e[1 - xh]
    copy_f.start()

    drain(recv_r.at[others], r_r)
    ranks = recv_r[:, 0, :]
    r = iota((capacity, owners), 0)
    expand = jnp.where(r // bucket == iota((capacity, owners), 1), 1.0, 0.0)
    spread = jnp.dot(expand, ranks, precision=lax.Precision.HIGHEST, preferred_element_type=F32)
    r = iota((capacity, 128), 0)
    lane = xh * side + core * bucket + r % bucket
    rank_col = jnp.sum(
        jnp.where(iota((capacity, 128), 1) == lane, spread, 0.0), axis=1, keepdims=True)
    eye = iota((capacity, capacity), 0) == iota((capacity, capacity), 1)
    rank_row = jnp.sum(jnp.where(eye, rank_col, 0.0), axis=0, keepdims=True)
    spot = me * bucket + slot_row
    pick = jnp.where(iota((128, rows), 0) == spot % 128, 1.0, 0.0)

    stage_d(xh)
    copy_e(xh).start()
    copy_f.wait_recv()
    copy_e(xh).wait_recv()
    total = gram[2 * xh + core] + recv_e[xh] + recv_f[...]
    diagonal = jnp.where(eye, total, 0.0)
    norm_row = lax.rsqrt(jnp.sum(diagonal, axis=0, keepdims=True) + 1e-06)
    norm_col = lax.rsqrt(jnp.sum(diagonal, axis=1, keepdims=True) + 1e-06)
    similarity = total * norm_col * norm_row
    highest = jnp.max(jnp.where(rank_col < rank_row, similarity, -2.0), axis=0, keepdims=True)
    highest = jnp.maximum(highest, -1.0)
    best_t[t] = jnp.broadcast_to(highest, (8, capacity))

    def copy_g(to, frm):
        return pltpu.make_async_remote_copy(
            best_t.at[frm], best_t.at[frm], g_s.at[to], g_r.at[frm], device_id=(me, to), device_id_type=MESH)

    for o in range(1, 4):
        copy_g(lax.rem(t + o, 4), t).start()
    for o in range(1, 4):
        copy_g(t, lax.rem(t + o, 4)).wait_recv()
    line = iota((8, 128), 0)
    rows_h = jnp.zeros((8, 128), F32)
    for c in range(CLU_DEV):
        for j in range(2):
            rows_h = jnp.where(line == j * CLU_DEV + c, best_t[c, :, j * 128:(j + 1) * 128], rows_h)
    send_h[...] = rows_h
    each_peer(lambda to: pltpu.make_async_remote_copy(
        send_h, recv_h.at[me], h_s, h_r, device_id=(to, t), device_id_type=MESH).start())
    recv_h[me] = rows_h
    drain(recv_h.at[others], h_r)
    returned = recv_h[...].reshape(owners * 8, 128)
    found = jnp.dot(returned, pick, precision=lax.Precision.HIGHEST, preferred_element_type=F32)
    where = (cluster_row // CLU_DEV) * 8 + (spot // 128) * CLU_DEV + cluster_row % CLU_DEV
    out_ref[...] = jnp.sum(
        jnp.where(iota((owners * 8, rows), 0) == where, found, 0.0), axis=0, keepdims=True)

    def sent_k(k, _):
        copy_a(k).wait_send()
        copy_b(k).wait_send()
        for h in range(2):
            drain(recv_c.at[k, h, others], c_s.at[k, h])
        return 0

    lax.fori_loop(0, chunks, sent_k, 0)
    drain(recv_r.at[others], r_s)
    drain(recv_h.at[others], h_s)
    copy_e(1 - xh).wait_send()
    copy_e(xh).wait_send()
    copy_f.wait_send()
    for o in range(1, 4):
        copy_g(lax.rem(t + o, 4), t).wait_send()


def shards(final_input, norm_gain, value_weight, out_weight, cluster, priority):
    rows, width = final_input.shape
    owners = lax.axis_size("dp")
    tensor = lax.axis_size("tensor")
    part = width // tensor
    chunk = part // CHUNKS
    bucket = max(2, 2 * rows // (CLU_DEV * owners))
    side = max(16, 2 * bucket)
    per_owner = 2 * side
    capacity = owners * bucket
    kv = value_weight.shape[1]
    vmem = pl.BlockSpec(memory_space=pltpu.VMEM)
    anywhere = pl.BlockSpec(memory_space=pl.ANY)
    dma = pltpu.SemaphoreType.DMA
    best = pl.pallas_call(
        functools.partial(kernel, owners, bucket),
        out_shape=jax.ShapeDtypeStruct((1, rows), F32),
        in_specs=[anywhere, vmem, anywhere, anywhere, vmem, vmem],
        out_specs=vmem,
        scratch_shapes=[
            pltpu.VMEM((rows, width), BF16),
            pltpu.VMEM((width, kv), BF16),
            pltpu.VMEM(out_weight.shape, BF16),
            pltpu.VMEM((rows, 1), F32),
            pltpu.VMEM((rows, kv), BF16),
            pltpu.VMEM((CHUNKS, 2, rows, chunk), BF16),
            pltpu.VMEM((CHUNKS, 2, rows, chunk), BF16),
            pltpu.VMEM((CHUNKS, 2, rows, chunk), BF16),
            pltpu.VMEM((CHUNKS, rows, chunk), BF16),
            pltpu.VMEM((CHUNKS, rows, chunk), BF16),
            pltpu.VMEM((owners * per_owner, rows), BF16),
            pltpu.VMEM((CHUNKS, owners, 2, side, chunk), BF16),
            pltpu.VMEM((CHUNKS, 2, owners, side, chunk), BF16),
            pltpu.VMEM((owners, 8, 128), F32),
            pltpu.VMEM((owners, 8, 128), F32),
            pltpu.VMEM((CLU_DEV, capacity, capacity), F32),
            pltpu.VMEM((2, capacity, capacity), F32),
            pltpu.VMEM((capacity, capacity), F32),
            pltpu.VMEM((capacity, capacity), F32),
            pltpu.VMEM((CLU_DEV, 8, capacity), F32),
            pltpu.VMEM((8, 128), F32),
            pltpu.VMEM((owners, 8, 128), F32),
            dma((4,)),
            dma((CHUNKS,)), dma((CHUNKS,)),
            dma((CHUNKS,)), dma((CHUNKS,)),
            dma((CHUNKS, 2)), dma((CHUNKS, 2)),
            dma, dma,
            dma((2,)), dma((2,)),
            dma, dma,
            dma((4,)), dma((4,)),
            dma, dma,
        ],
        compiler_params=pltpu.CompilerParams(
            collective_id=0, has_side_effects=True, vmem_limit_bytes=56 * 1024 * 1024),
        cost_estimate=pl.CostEstimate(flops=6_000_000_000, bytes_accessed=16_000_000, transcendentals=0),
    )(final_input, norm_gain, value_weight, out_weight, cluster.reshape(1, rows), priority.reshape(1, rows))
    return best.reshape(rows)


def solution(mesh):
    in_specs = (P("dp", None), P(), P(None, "tensor"), P("tensor", None), P("dp", None), P("dp"))
    out_specs = P("dp")
    return jax.shard_map(shards, mesh=mesh, in_specs=in_specs, out_specs=out_specs, check_vma=False)
```

```python
import functools

import jax
import jax.numpy as jnp
from jax import lax
from jax.experimental import pallas as pl
from jax.experimental.pallas import tpu as pltpu
from jax.sharding import PartitionSpec as P

HEADS = 32
KV_HEADS = 8
HEAD_DIM = 128
CLU_DEV = 4
CHUNKS = 8
LAG = 5
MESH = pl.DeviceIdType.MESH
BF16 = jnp.bfloat16
F32 = jnp.float32
I32 = jnp.int32


def iota(shape, dim):
    return lax.broadcasted_iota(I32, shape, dim)


def drain(ref, sem):
    pltpu.make_async_copy(ref, ref, sem).wait()


def kernel(
    owners, bucket,
    x_hbm, gain_ref, vw_hbm, ow_hbm, cluster_ref, priority_ref, out_ref,
    x_v, vw_v, ow_v, scale_v, values, send_a, keep_a, recv_a, send_b, recv_b,
    place, send_c, recv_c, send_r, recv_r, gram, recv_e, send_f, recv_f, best_t, send_h, recv_h,
    in_sem, a_s, a_r, b_s, b_r, c_s, c_r, r_s, r_r, e_s, e_r, f_s, f_r, g_s, g_r, h_s, h_r,
):
    rows, width = x_v.shape
    chunks, _, chunk = recv_b.shape
    part = chunk * chunks
    side = recv_c.shape[3]
    per_owner = 2 * side
    capacity = owners * bucket
    sentinel = owners * rows
    me = lax.axis_index("dp")
    t = lax.axis_index("tensor")
    xh, core = t // 2, t % 2
    partner = 2 * xh + (1 - core)
    across = 2 * (1 - xh) + core
    half = rows // 2

    def peer(o):
        found, bit = 0, 1
        while bit < owners:
            found = found + lax.rem(me // bit + o // bit, 2) * bit
            bit = 2 * bit
        return found

    def each_peer(act):
        def step(i, _):
            act(peer(owners - 1 - i))
            return 0

        lax.fori_loop(0, owners - 1, step, 0)

    def load_x(i):
        span = pl.ds(i * half, half)
        return pltpu.make_async_copy(x_hbm.at[span], x_v.at[span], in_sem.at[i])

    load_vw = pltpu.make_async_copy(vw_hbm, vw_v, in_sem.at[2])

    def load_ow(start, size, sem):
        for q in range(4):
            span = pl.ds(q * part + start, size)
            pltpu.make_async_copy(ow_hbm.at[:, span], ow_v.at[:, span], sem).start()

    load_x(0).start()
    load_vw.start()
    load_x(1).start()
    load_ow(0, chunk, in_sem.at[3])

    barrier = pltpu.get_barrier_semaphore()
    for o in range(1, 4):
        pl.semaphore_signal(barrier, inc=1, device_id=(me, lax.rem(t + o, 4)), device_id_type=MESH)
    each_peer(lambda to: pl.semaphore_signal(barrier, inc=1, device_id=(to, t), device_id_type=MESH))

    cluster_row = cluster_ref[...]
    square = (rows, rows)
    i0, i1 = iota(square, 0), iota(square, 1)
    cluster_col = jnp.sum(jnp.where(i0 == i1, cluster_row, 0), axis=1, keepdims=True)
    slot_row = jnp.sum(
        jnp.where((cluster_col == cluster_row) & (i0 < i1), 1, 0), axis=0, keepdims=True)
    flat_row = (cluster_row // 2) * side + (cluster_row % 2) * bucket + slot_row
    place[...] = jnp.where(iota(place.shape, 0) == flat_row, 1.0, 0.0).astype(BF16)

    def project(i):
        span = pl.ds(i * half, half)
        xs = x_v[span, :]
        gained = xs * gain_ref[...].reshape(1, width)
        values[span, :] = jnp.dot(gained, vw_v[...], preferred_element_type=F32).astype(BF16)

    load_x(0).wait()
    load_vw.wait()
    load_ow(chunk, part - chunk, in_sem.at[4])
    project(0)
    load_x(1).wait()
    project(1)
    drain(ow_v.at[:, pl.ds(0, 4 * chunk)], in_sem.at[3])
    pl.semaphore_wait(barrier, 3 + owners - 1)

    def copy_a(k):
        return pltpu.make_async_remote_copy(
            send_a.at[k], recv_a.at[k], a_s.at[k], a_r.at[k], device_id=(me, partner), device_id_type=MESH)

    def copy_b(k):
        return pltpu.make_async_remote_copy(
            send_b.at[k], recv_b.at[k], b_s.at[k], b_r.at[k], device_id=(me, across), device_id_type=MESH)

    def start_c(k, h):
        each_peer(lambda to: pltpu.make_async_remote_copy(
            send_c.at[k, to, h], recv_c.at[k, h, me], c_s.at[k, h], c_r.at[k, h],
            device_id=(to, t), device_id_type=MESH).start())
        recv_c[k, h, me] = send_c[k, me, h]

    def term(quarter, k):
        columns = pl.ds(pl.multiple_of(quarter * part + k * chunk, chunk), chunk)
        w = ow_v[:, columns].astype(F32)
        kv_local = values.shape[1] // HEAD_DIM
        w = w.reshape(kv_local, HEADS // KV_HEADS, HEAD_DIM, chunk)
        w = jnp.sum(w, axis=1).reshape(kv_local * HEAD_DIM, chunk).astype(BF16)
        return jnp.dot(values[...], w, preferred_element_type=F32).astype(BF16)

    def stage_a(k):
        for h in range(2):
            send_a[k, h] = term(2 * h + 1 - core, k)
        copy_a(k).start()
        for h in range(2):
            keep_a[k, h] = term(2 * h + core, k)

    def stage_b(k):
        copy_a(k).wait_recv()
        send_b[k] = (keep_a[k, 1 - xh].astype(F32) + recv_a[k, 1 - xh].astype(F32)).astype(BF16)
        copy_b(k).start()

    def stage_c(k):
        copy_b(k).wait_recv()
        columns = pl.ds(pl.multiple_of(t * part + k * chunk, chunk), chunk)
        attention = keep_a[k, xh].astype(F32) + recv_a[k, xh].astype(F32) + recv_b[k].astype(F32)
        hidden = (x_v[:, columns].astype(F32) + attention * scale_v[...]).astype(BF16)
        placed = jnp.dot(place[...], hidden, preferred_element_type=F32).astype(BF16)
        send_c[k] = placed.reshape(owners, 2, side, chunk)
        start_c(k, 1 - xh)

        @pl.when(k % 2 == 0)
        def _():
            start_c(k // 2, xh)

    def step(s, _):
        @pl.when(s == 1)
        def _():
            drain(ow_v.at[:, pl.ds(0, 4 * (part - chunk))], in_sem.at[4])

        @pl.when(s < chunks)
        def _():
            stage_a(s)

        @pl.when((s > 0) & (s <= chunks))
        def _():
            stage_b(s - 1)

        @pl.when(s >= LAG)
        def _():
            stage_c(s - LAG)

        return 0

    lax.fori_loop(0, 2, step, 0)

    def row_scale(i, _):
        span = pl.ds(pl.multiple_of(i * 128, 128), 128)
        xs = x_v[span, :].astype(F32)
        scale_v[span, :] = lax.rsqrt(jnp.sum(xs * xs, axis=1, keepdims=True) * (1.0 / width) + 1e-05)
        return 0

    lax.fori_loop(0, rows // 128, row_scale, 0)
    rank = priority_ref[...]
    high, low = (rank // 128).astype(F32), (rank % 128).astype(F32)
    line = iota((8, rows), 0)
    meta = jnp.where(line == 0, high, jnp.where(line == 1, low, jnp.where(line == 2, 1.0, 0.0)))
    meta = meta.astype(BF16)

    def rank_block(to, _):
        s = iota((128, rows), 0)
        hit = (s + to * per_owner == flat_row) & (s < per_owner)
        got = lax.dot_general(
            meta, jnp.where(hit, 1.0, 0.0).astype(BF16), (((1,), (1,)), ((), ())),
            preferred_element_type=F32)
        line = got[0:1] * 128.0 + got[1:2] + (1.0 - got[2:3]) * float(sentinel)
        send_r[to] = jnp.broadcast_to(line, (8, 128))
        return 0

    lax.fori_loop(0, owners, rank_block, 0)
    recv_r[me] = send_r[me]
    each_peer(lambda to: pltpu.make_async_remote_copy(
        send_r.at[to], recv_r.at[me], r_s, r_r, device_id=(to, t), device_id_type=MESH).start())

    lax.fori_loop(2, chunks + LAG, step, 0)
    lax.fori_loop(chunks // 2, chunks, lambda k, _: start_c(k, xh) or 0, 0)
    others = pl.ds(0, owners - 1)
    gram[...] = jnp.zeros_like(gram)

    def stage_d(h):
        def one(k, _):
            drain(recv_c.at[k, h, others], c_r.at[k, h])
            for c in range(2):
                if bucket % 16 == 0:
                    members = recv_c[k, h, :, c * bucket:(c + 1) * bucket, :].reshape(capacity, chunk)
                else:
                    every = recv_c[k, h].reshape(owners * side, chunk)
                    shape = (capacity, owners * side)
                    r = iota(shape, 0)
                    pick = (r // bucket) * side + c * bucket + r % bucket == iota(shape, 1)
                    members = jnp.dot(
                        jnp.where(pick, 1.0, 0.0).astype(BF16), every, preferred_element_type=F32)
                    members = members.astype(BF16)
                gram[2 * h + c] += lax.dot_general(
                    members, members, (((1,), (1,)), ((), ())), preferred_element_type=F32)
            return 0

        lax.fori_loop(0, chunks, one, 0)

    def copy_e(h):
        return pltpu.make_async_remote_copy(
            gram.at[2 * h + 1 - core], recv_e.at[h], e_s.at[h], e_r.at[h],
            device_id=(me, partner), device_id_type=MESH)

    copy_f = pltpu.make_async_remote_copy(
        send_f, recv_f, f_s, f_r, device_id=(me, across), device_id_type=MESH)

    stage_d(1 - xh)
    copy_e(1 - xh).start()
    copy_e(1 - xh).wait_recv()
    send_f[...] = gram[2 * (1 - xh) + core] + recv_e[1 - xh]
    copy_f.start()

    drain(recv_r.at[others], r_r)
    ranks = recv_r[:, 0, :]
    r = iota((capacity, owners), 0)
    expand = jnp.where(r // bucket == iota((capacity, owners), 1), 1.0, 0.0)
    spread = jnp.dot(expand, ranks, precision=lax.Precision.HIGHEST, preferred_element_type=F32)
    r = iota((capacity, 128), 0)
    lane = xh * side + core * bucket + r % bucket
    rank_col = jnp.sum(
        jnp.where(iota((capacity, 128), 1) == lane, spread, 0.0), axis=1, keepdims=True)
    eye = iota((capacity, capacity), 0) == iota((capacity, capacity), 1)
    rank_row = jnp.sum(jnp.where(eye, rank_col, 0.0), axis=0, keepdims=True)
    spot = me * bucket + slot_row
    pick = jnp.where(iota((128, rows), 0) == spot % 128, 1.0, 0.0)

    stage_d(xh)
    copy_e(xh).start()
    copy_f.wait_recv()
    copy_e(xh).wait_recv()
    total = gram[2 * xh + core] + recv_e[xh] + recv_f[...]
    diagonal = jnp.where(eye, total, 0.0)
    norm_row = lax.rsqrt(jnp.sum(diagonal, axis=0, keepdims=True) + 1e-06)
    norm_col = lax.rsqrt(jnp.sum(diagonal, axis=1, keepdims=True) + 1e-06)
    similarity = total * norm_col * norm_row
    highest = jnp.max(jnp.where(rank_col < rank_row, similarity, -2.0), axis=0, keepdims=True)
    highest = jnp.maximum(highest, -1.0)
    best_t[t] = jnp.broadcast_to(highest, (8, capacity))

    def copy_g(to, frm):
        return pltpu.make_async_remote_copy(
            best_t.at[frm], best_t.at[frm], g_s.at[to], g_r.at[frm], device_id=(me, to), device_id_type=MESH)

    for o in range(1, 4):
        copy_g(lax.rem(t + o, 4), t).start()
    for o in range(1, 4):
        copy_g(t, lax.rem(t + o, 4)).wait_recv()
    line = iota((8, 128), 0)
    rows_h = jnp.zeros((8, 128), F32)
    for c in range(CLU_DEV):
        for j in range(2):
            rows_h = jnp.where(line == j * CLU_DEV + c, best_t[c, :, j * 128:(j + 1) * 128], rows_h)
    send_h[...] = rows_h
    each_peer(lambda to: pltpu.make_async_remote_copy(
        send_h, recv_h.at[me], h_s, h_r, device_id=(to, t), device_id_type=MESH).start())
    recv_h[me] = rows_h
    drain(recv_h.at[others], h_r)
    returned = recv_h[...].reshape(owners * 8, 128)
    found = jnp.dot(returned, pick, precision=lax.Precision.HIGHEST, preferred_element_type=F32)
    where = (cluster_row // CLU_DEV) * 8 + (spot // 128) * CLU_DEV + cluster_row % CLU_DEV
    out_ref[...] = jnp.sum(
        jnp.where(iota((owners * 8, rows), 0) == where, found, 0.0), axis=0, keepdims=True)

    def sent_k(k, _):
        copy_a(k).wait_send()
        copy_b(k).wait_send()
        for h in range(2):
            drain(recv_c.at[k, h, others], c_s.at[k, h])
        return 0

    lax.fori_loop(0, chunks, sent_k, 0)
    drain(recv_r.at[others], r_s)
    drain(recv_h.at[others], h_s)
    copy_e(1 - xh).wait_send()
    copy_e(xh).wait_send()
    copy_f.wait_send()
    for o in range(1, 4):
        copy_g(lax.rem(t + o, 4), t).wait_send()


def shards(final_input, norm_gain, value_weight, out_weight, cluster, priority):
    rows, width = final_input.shape
    owners = lax.axis_size("dp")
    tensor = lax.axis_size("tensor")
    part = width // tensor
    chunk = part // CHUNKS
    bucket = max(2, 2 * rows // (CLU_DEV * owners))
    side = max(16, 2 * bucket)
    per_owner = 2 * side
    capacity = owners * bucket
    kv = value_weight.shape[1]
    vmem = pl.BlockSpec(memory_space=pltpu.VMEM)
    anywhere = pl.BlockSpec(memory_space=pl.ANY)
    dma = pltpu.SemaphoreType.DMA
    best = pl.pallas_call(
        functools.partial(kernel, owners, bucket),
        out_shape=jax.ShapeDtypeStruct((1, rows), F32),
        in_specs=[anywhere, vmem, anywhere, anywhere, vmem, vmem],
        out_specs=vmem,
        scratch_shapes=[
            pltpu.VMEM((rows, width), BF16),
            pltpu.VMEM((width, kv), BF16),
            pltpu.VMEM(out_weight.shape, BF16),
            pltpu.VMEM((rows, 1), F32),
            pltpu.VMEM((rows, kv), BF16),
            pltpu.VMEM((CHUNKS, 2, rows, chunk), BF16),
            pltpu.VMEM((CHUNKS, 2, rows, chunk), BF16),
            pltpu.VMEM((CHUNKS, 2, rows, chunk), BF16),
            pltpu.VMEM((CHUNKS, rows, chunk), BF16),
            pltpu.VMEM((CHUNKS, rows, chunk), BF16),
            pltpu.VMEM((owners * per_owner, rows), BF16),
            pltpu.VMEM((CHUNKS, owners, 2, side, chunk), BF16),
            pltpu.VMEM((CHUNKS, 2, owners, side, chunk), BF16),
            pltpu.VMEM((owners, 8, 128), F32),
            pltpu.VMEM((owners, 8, 128), F32),
            pltpu.VMEM((CLU_DEV, capacity, capacity), F32),
            pltpu.VMEM((2, capacity, capacity), F32),
            pltpu.VMEM((capacity, capacity), F32),
            pltpu.VMEM((capacity, capacity), F32),
            pltpu.VMEM((CLU_DEV, 8, capacity), F32),
            pltpu.VMEM((8, 128), F32),
            pltpu.VMEM((owners, 8, 128), F32),
            dma((5,)),
            dma((CHUNKS,)), dma((CHUNKS,)),
            dma((CHUNKS,)), dma((CHUNKS,)),
            dma((CHUNKS, 2)), dma((CHUNKS, 2)),
            dma, dma,
            dma((2,)), dma((2,)),
            dma, dma,
            dma((4,)), dma((4,)),
            dma, dma,
        ],
        compiler_params=pltpu.CompilerParams(
            collective_id=0, has_side_effects=True, vmem_limit_bytes=56 * 1024 * 1024),
        cost_estimate=pl.CostEstimate(flops=6_000_000_000, bytes_accessed=16_000_000, transcendentals=0),
    )(final_input, norm_gain, value_weight, out_weight, cluster.reshape(1, rows), priority.reshape(1, rows))
    return best.reshape(rows)


def solution(mesh):
    in_specs = (P("dp", None), P(), P(None, "tensor"), P("tensor", None), P("dp", None), P("dp"))
    out_specs = P("dp")
    return jax.shard_map(shards, mesh=mesh, in_specs=in_specs, out_specs=out_specs, check_vma=False)
```

```python
import functools

import jax
import jax.numpy as jnp
from jax import lax
from jax.experimental import pallas as pl
from jax.experimental.pallas import tpu as pltpu
from jax.sharding import PartitionSpec as P

HEADS = 32
KV_HEADS = 8
HEAD_DIM = 128
CLU_DEV = 4
CHUNKS = 8
LAG = 2
HELD = 2
MESH = pl.DeviceIdType.MESH
BF16 = jnp.bfloat16
F32 = jnp.float32
I32 = jnp.int32


def iota(shape, dim):
    return lax.broadcasted_iota(I32, shape, dim)


def drain(ref, sem):
    pltpu.make_async_copy(ref, ref, sem).wait()


def kernel(
    owners, bucket,
    x_hbm, gain_ref, vw_hbm, ow_hbm, cluster_ref, priority_ref, out_ref,
    x_v, vw_v, ow_v, scale_v, values, send_a, keep_a, recv_a, send_b, recv_b,
    place, send_c, recv_c, send_r, recv_r, gram, recv_e, send_f, recv_f, best_t, send_h, recv_h,
    in_sem, a_s, a_r, b_s, b_r, c_s, c_r, r_s, r_r, e_s, e_r, f_s, f_r, g_s, g_r, h_s, h_r,
):
    rows, width = x_v.shape
    chunks, _, chunk = recv_b.shape
    part = chunk * chunks
    side = recv_c.shape[3]
    per_owner = 2 * side
    capacity = owners * bucket
    sentinel = owners * rows
    me = lax.axis_index("dp")
    t = lax.axis_index("tensor")
    xh, core = t // 2, t % 2
    partner = 2 * xh + (1 - core)
    across = 2 * (1 - xh) + core
    half = rows // 2

    def peer(o):
        found, bit = 0, 1
        while bit < owners:
            found = found + lax.rem(me // bit + o // bit, 2) * bit
            bit = 2 * bit
        return found

    def each_peer(act):
        def step(i, _):
            act(peer(owners - 1 - i))
            return 0

        lax.fori_loop(0, owners - 1, step, 0)

    def load_x(i):
        span = pl.ds(i * half, half)
        return pltpu.make_async_copy(x_hbm.at[span], x_v.at[span], in_sem.at[i])

    load_vw = pltpu.make_async_copy(vw_hbm, vw_v, in_sem.at[2])

    def load_ow(start, size, sem):
        for q in range(4):
            span = pl.ds(q * part + start, size)
            pltpu.make_async_copy(ow_hbm.at[:, span], ow_v.at[:, span], sem).start()

    load_x(0).start()
    load_vw.start()
    load_x(1).start()
    load_ow(0, chunk, in_sem.at[3])

    barrier = pltpu.get_barrier_semaphore()
    for o in range(1, 4):
        pl.semaphore_signal(barrier, inc=1, device_id=(me, lax.rem(t + o, 4)), device_id_type=MESH)
    each_peer(lambda to: pl.semaphore_signal(barrier, inc=1, device_id=(to, t), device_id_type=MESH))

    cluster_row = cluster_ref[...]
    square = (rows, rows)
    i0, i1 = iota(square, 0), iota(square, 1)
    cluster_col = jnp.sum(jnp.where(i0 == i1, cluster_row, 0), axis=1, keepdims=True)
    slot_row = jnp.sum(
        jnp.where((cluster_col == cluster_row) & (i0 < i1), 1, 0), axis=0, keepdims=True)
    flat_row = (cluster_row // 2) * side + (cluster_row % 2) * bucket + slot_row
    place[...] = jnp.where(iota(place.shape, 0) == flat_row, 1.0, 0.0).astype(BF16)

    def project(i):
        span = pl.ds(i * half, half)
        xs = x_v[span, :]
        gained = xs * gain_ref[...].reshape(1, width)
        values[span, :] = jnp.dot(gained, vw_v[...], preferred_element_type=F32).astype(BF16)

    load_x(0).wait()
    load_vw.wait()
    load_ow(chunk, part - chunk, in_sem.at[4])
    project(0)
    load_x(1).wait()
    project(1)
    drain(ow_v.at[:, pl.ds(0, 4 * chunk)], in_sem.at[3])
    pl.semaphore_wait(barrier, 3 + owners - 1)

    def copy_a(k):
        return pltpu.make_async_remote_copy(
            send_a.at[k], recv_a.at[k], a_s.at[k], a_r.at[k], device_id=(me, partner), device_id_type=MESH)

    def copy_b(k):
        return pltpu.make_async_remote_copy(
            send_b.at[k], recv_b.at[k], b_s.at[k], b_r.at[k], device_id=(me, across), device_id_type=MESH)

    def start_c(k, h):
        each_peer(lambda to: pltpu.make_async_remote_copy(
            send_c.at[k, to, h], recv_c.at[k, h, me], c_s.at[k, h], c_r.at[k, h],
            device_id=(to, t), device_id_type=MESH).start())
        recv_c[k, h, me] = send_c[k, me, h]

    def term(quarter, k):
        columns = pl.ds(pl.multiple_of(quarter * part + k * chunk, chunk), chunk)
        w = ow_v[:, columns].astype(F32)
        kv_local = values.shape[1] // HEAD_DIM
        w = w.reshape(kv_local, HEADS // KV_HEADS, HEAD_DIM, chunk)
        w = jnp.sum(w, axis=1).reshape(kv_local * HEAD_DIM, chunk).astype(BF16)
        return jnp.dot(values[...], w, preferred_element_type=F32).astype(BF16)

    def stage_a(k):
        for h in range(2):
            send_a[k, h] = term(2 * h + 1 - core, k)
        copy_a(k).start()
        for h in range(2):
            keep_a[k, h] = term(2 * h + core, k)

    def stage_b(k):
        copy_a(k).wait_recv()
        send_b[k] = (keep_a[k, 1 - xh].astype(F32) + recv_a[k, 1 - xh].astype(F32)).astype(BF16)
        copy_b(k).start()

    def stage_c(k):
        copy_b(k).wait_recv()
        columns = pl.ds(pl.multiple_of(t * part + k * chunk, chunk), chunk)
        attention = keep_a[k, xh].astype(F32) + recv_a[k, xh].astype(F32) + recv_b[k].astype(F32)
        hidden = (x_v[:, columns].astype(F32) + attention * scale_v[...]).astype(BF16)
        placed = jnp.dot(place[...], hidden, preferred_element_type=F32).astype(BF16)
        send_c[k] = placed.reshape(owners, 2, side, chunk)
        start_c(k, 1 - xh)

        @pl.when(k % 2 == 0)
        def _():
            start_c(k // 2, xh)

    def step(s, _):
        @pl.when(s == 1)
        def _():
            drain(ow_v.at[:, pl.ds(0, 4 * (part - chunk))], in_sem.at[4])

        @pl.when(s < chunks)
        def _():
            stage_a(s)

        @pl.when((s > 0) & (s <= chunks))
        def _():
            stage_b(s - 1)

        @pl.when(s >= LAG)
        def _():
            stage_c(s - LAG)

        return 0

    lax.fori_loop(0, 2, step, 0)

    def row_scale(i, _):
        span = pl.ds(pl.multiple_of(i * 128, 128), 128)
        xs = x_v[span, :].astype(F32)
        scale_v[span, :] = lax.rsqrt(jnp.sum(xs * xs, axis=1, keepdims=True) * (1.0 / width) + 1e-05)
        return 0

    lax.fori_loop(0, rows // 128, row_scale, 0)
    rank = priority_ref[...]
    high, low = (rank // 128).astype(F32), (rank % 128).astype(F32)
    line = iota((8, rows), 0)
    meta = jnp.where(line == 0, high, jnp.where(line == 1, low, jnp.where(line == 2, 1.0, 0.0)))
    meta = meta.astype(BF16)

    def rank_block(to, _):
        s = iota((128, rows), 0)
        hit = (s + to * per_owner == flat_row) & (s < per_owner)
        got = lax.dot_general(
            meta, jnp.where(hit, 1.0, 0.0).astype(BF16), (((1,), (1,)), ((), ())),
            preferred_element_type=F32)
        line = got[0:1] * 128.0 + got[1:2] + (1.0 - got[2:3]) * float(sentinel)
        send_r[to] = jnp.broadcast_to(line, (8, 128))
        return 0

    lax.fori_loop(0, owners, rank_block, 0)
    recv_r[me] = send_r[me]
    each_peer(lambda to: pltpu.make_async_remote_copy(
        send_r.at[to], recv_r.at[me], r_s, r_r, device_id=(to, t), device_id_type=MESH).start())

    lax.fori_loop(2, chunks + LAG, step, 0)
    lax.fori_loop(chunks // 2, chunks - HELD, lambda k, _: start_c(k, xh) or 0, 0)
    others = pl.ds(0, owners - 1)
    gram[...] = jnp.zeros_like(gram)

    def stage_d(h):
        def one(k, _):
            drain(recv_c.at[k, h, others], c_r.at[k, h])
            for c in range(2):
                if bucket % 16 == 0:
                    members = recv_c[k, h, :, c * bucket:(c + 1) * bucket, :].reshape(capacity, chunk)
                else:
                    every = recv_c[k, h].reshape(owners * side, chunk)
                    shape = (capacity, owners * side)
                    r = iota(shape, 0)
                    pick = (r // bucket) * side + c * bucket + r % bucket == iota(shape, 1)
                    members = jnp.dot(
                        jnp.where(pick, 1.0, 0.0).astype(BF16), every, preferred_element_type=F32)
                    members = members.astype(BF16)
                gram[2 * h + c] += lax.dot_general(
                    members, members, (((1,), (1,)), ((), ())), preferred_element_type=F32)
            return 0

        lax.fori_loop(0, chunks, one, 0)

    def copy_e(h):
        return pltpu.make_async_remote_copy(
            gram.at[2 * h + 1 - core], recv_e.at[h], e_s.at[h], e_r.at[h],
            device_id=(me, partner), device_id_type=MESH)

    copy_f = pltpu.make_async_remote_copy(
        send_f, recv_f, f_s, f_r, device_id=(me, across), device_id_type=MESH)

    stage_d(1 - xh)
    copy_e(1 - xh).start()
    copy_e(1 - xh).wait_recv()
    send_f[...] = gram[2 * (1 - xh) + core] + recv_e[1 - xh]
    copy_f.start()
    lax.fori_loop(chunks - HELD, chunks, lambda k, _: start_c(k, xh) or 0, 0)

    drain(recv_r.at[others], r_r)
    ranks = recv_r[:, 0, :]
    r = iota((capacity, owners), 0)
    expand = jnp.where(r // bucket == iota((capacity, owners), 1), 1.0, 0.0)
    spread = jnp.dot(expand, ranks, precision=lax.Precision.HIGHEST, preferred_element_type=F32)
    r = iota((capacity, 128), 0)
    lane = xh * side + core * bucket + r % bucket
    rank_col = jnp.sum(
        jnp.where(iota((capacity, 128), 1) == lane, spread, 0.0), axis=1, keepdims=True)
    eye = iota((capacity, capacity), 0) == iota((capacity, capacity), 1)
    rank_row = jnp.sum(jnp.where(eye, rank_col, 0.0), axis=0, keepdims=True)
    spot = me * bucket + slot_row
    pick = jnp.where(iota((128, rows), 0) == spot % 128, 1.0, 0.0)

    stage_d(xh)
    copy_e(xh).start()
    copy_f.wait_recv()
    copy_e(xh).wait_recv()
    total = gram[2 * xh + core] + recv_e[xh] + recv_f[...]
    diagonal = jnp.where(eye, total, 0.0)
    norm_row = lax.rsqrt(jnp.sum(diagonal, axis=0, keepdims=True) + 1e-06)
    norm_col = lax.rsqrt(jnp.sum(diagonal, axis=1, keepdims=True) + 1e-06)
    similarity = total * norm_col * norm_row
    highest = jnp.max(jnp.where(rank_col < rank_row, similarity, -2.0), axis=0, keepdims=True)
    highest = jnp.maximum(highest, -1.0)
    best_t[t] = jnp.broadcast_to(highest, (8, capacity))

    def copy_g(to, frm):
        return pltpu.make_async_remote_copy(
            best_t.at[frm], best_t.at[frm], g_s.at[to], g_r.at[frm], device_id=(me, to), device_id_type=MESH)

    for o in range(1, 4):
        copy_g(lax.rem(t + o, 4), t).start()
    for o in range(1, 4):
        copy_g(t, lax.rem(t + o, 4)).wait_recv()
    line = iota((8, 128), 0)
    rows_h = jnp.zeros((8, 128), F32)
    for c in range(CLU_DEV):
        for j in range(2):
            rows_h = jnp.where(line == j * CLU_DEV + c, best_t[c, :, j * 128:(j + 1) * 128], rows_h)
    send_h[...] = rows_h
    each_peer(lambda to: pltpu.make_async_remote_copy(
        send_h, recv_h.at[me], h_s, h_r, device_id=(to, t), device_id_type=MESH).start())
    recv_h[me] = rows_h
    drain(recv_h.at[others], h_r)
    returned = recv_h[...].reshape(owners * 8, 128)
    found = jnp.dot(returned, pick, precision=lax.Precision.HIGHEST, preferred_element_type=F32)
    where = (cluster_row // CLU_DEV) * 8 + (spot // 128) * CLU_DEV + cluster_row % CLU_DEV
    out_ref[...] = jnp.sum(
        jnp.where(iota((owners * 8, rows), 0) == where, found, 0.0), axis=0, keepdims=True)

    def sent_k(k, _):
        copy_a(k).wait_send()
        copy_b(k).wait_send()
        for h in range(2):
            drain(recv_c.at[k, h, others], c_s.at[k, h])
        return 0

    lax.fori_loop(0, chunks, sent_k, 0)
    drain(recv_r.at[others], r_s)
    drain(recv_h.at[others], h_s)
    copy_e(1 - xh).wait_send()
    copy_e(xh).wait_send()
    copy_f.wait_send()
    for o in range(1, 4):
        copy_g(lax.rem(t + o, 4), t).wait_send()


def shards(final_input, norm_gain, value_weight, out_weight, cluster, priority):
    rows, width = final_input.shape
    owners = lax.axis_size("dp")
    tensor = lax.axis_size("tensor")
    part = width // tensor
    chunk = part // CHUNKS
    bucket = max(2, 2 * rows // (CLU_DEV * owners))
    side = max(16, 2 * bucket)
    per_owner = 2 * side
    capacity = owners * bucket
    kv = value_weight.shape[1]
    vmem = pl.BlockSpec(memory_space=pltpu.VMEM)
    anywhere = pl.BlockSpec(memory_space=pl.ANY)
    dma = pltpu.SemaphoreType.DMA
    best = pl.pallas_call(
        functools.partial(kernel, owners, bucket),
        out_shape=jax.ShapeDtypeStruct((1, rows), F32),
        in_specs=[anywhere, vmem, anywhere, anywhere, vmem, vmem],
        out_specs=vmem,
        scratch_shapes=[
            pltpu.VMEM((rows, width), BF16),
            pltpu.VMEM((width, kv), BF16),
            pltpu.VMEM(out_weight.shape, BF16),
            pltpu.VMEM((rows, 1), F32),
            pltpu.VMEM((rows, kv), BF16),
            pltpu.VMEM((CHUNKS, 2, rows, chunk), BF16),
            pltpu.VMEM((CHUNKS, 2, rows, chunk), BF16),
            pltpu.VMEM((CHUNKS, 2, rows, chunk), BF16),
            pltpu.VMEM((CHUNKS, rows, chunk), BF16),
            pltpu.VMEM((CHUNKS, rows, chunk), BF16),
            pltpu.VMEM((owners * per_owner, rows), BF16),
            pltpu.VMEM((CHUNKS, owners, 2, side, chunk), BF16),
            pltpu.VMEM((CHUNKS, 2, owners, side, chunk), BF16),
            pltpu.VMEM((owners, 8, 128), F32),
            pltpu.VMEM((owners, 8, 128), F32),
            pltpu.VMEM((CLU_DEV, capacity, capacity), F32),
            pltpu.VMEM((2, capacity, capacity), F32),
            pltpu.VMEM((capacity, capacity), F32),
            pltpu.VMEM((capacity, capacity), F32),
            pltpu.VMEM((CLU_DEV, 8, capacity), F32),
            pltpu.VMEM((8, 128), F32),
            pltpu.VMEM((owners, 8, 128), F32),
            dma((5,)),
            dma((CHUNKS,)), dma((CHUNKS,)),
            dma((CHUNKS,)), dma((CHUNKS,)),
            dma((CHUNKS, 2)), dma((CHUNKS, 2)),
            dma, dma,
            dma((2,)), dma((2,)),
            dma, dma,
            dma((4,)), dma((4,)),
            dma, dma,
        ],
        compiler_params=pltpu.CompilerParams(
            collective_id=0, has_side_effects=True, vmem_limit_bytes=56 * 1024 * 1024),
        cost_estimate=pl.CostEstimate(flops=6_000_000_000, bytes_accessed=16_000_000, transcendentals=0),
    )(final_input, norm_gain, value_weight, out_weight, cluster.reshape(1, rows), priority.reshape(1, rows))
    return best.reshape(rows)


def solution(mesh):
    in_specs = (P("dp", None), P(), P(None, "tensor"), P("tensor", None), P("dp", None), P("dp"))
    out_specs = P("dp")
    return jax.shard_map(shards, mesh=mesh, in_specs=in_specs, out_specs=out_specs, check_vma=False)
```

```python
import functools

import jax
import jax.numpy as jnp
from jax import lax
from jax.experimental import pallas as pl
from jax.experimental.pallas import tpu as pltpu
from jax.sharding import PartitionSpec as P

HEADS = 32
KV_HEADS = 8
HEAD_DIM = 128
CLU_DEV = 4
CHUNKS = 8
LAG = 2
HELD = 2
MESH = pl.DeviceIdType.MESH
BF16 = jnp.bfloat16
F32 = jnp.float32
I32 = jnp.int32


def iota(shape, dim):
    return lax.broadcasted_iota(I32, shape, dim)


def drain(ref, sem):
    pltpu.make_async_copy(ref, ref, sem).wait()


def kernel(
    owners, bucket,
    x_hbm, gain_ref, vw_hbm, ow_hbm, cluster_ref, priority_ref, out_ref,
    x_v, vw_v, ow_v, scale_v, values, send_a, keep_a, recv_a, send_b, recv_b,
    place, send_c, recv_c, send_r, recv_r, gram, recv_e, send_f, recv_f, best_t, send_h, recv_h,
    in_sem, a_s, a_r, b_s, b_r, c_s, c_r, r_s, r_r, e_s, e_r, f_s, f_r, g_s, g_r, h_s, h_r,
):
    rows, width = x_v.shape
    chunks, _, chunk = recv_b.shape
    part = chunk * chunks
    side = recv_c.shape[3]
    per_owner = 2 * side
    capacity = owners * bucket
    sentinel = owners * rows
    me = lax.axis_index("dp")
    t = lax.axis_index("tensor")
    xh, core = t // 2, t % 2
    partner = 2 * xh + (1 - core)
    across = 2 * (1 - xh) + core
    half = rows // 2

    def peer(o):
        found, bit = 0, 1
        while bit < owners:
            found = found + lax.rem(me // bit + o // bit, 2) * bit
            bit = 2 * bit
        return found

    turn = 2 * (2 * ((me // 2) % 2) + core)

    def each_peer(act):
        def step(i, _):
            act(peer(lax.rem(i + turn, owners - 1) + 1))
            return 0

        lax.fori_loop(0, owners - 1, step, 0)

    def load_x(i):
        span = pl.ds(i * half, half)
        return pltpu.make_async_copy(x_hbm.at[span], x_v.at[span], in_sem.at[i])

    load_vw = pltpu.make_async_copy(vw_hbm, vw_v, in_sem.at[2])

    def load_ow(start, size, sem):
        for q in range(4):
            span = pl.ds(q * part + start, size)
            pltpu.make_async_copy(ow_hbm.at[:, span], ow_v.at[:, span], sem).start()

    load_x(0).start()
    load_vw.start()
    load_x(1).start()
    load_ow(0, chunk, in_sem.at[3])

    barrier = pltpu.get_barrier_semaphore()
    for o in range(1, 4):
        pl.semaphore_signal(barrier, inc=1, device_id=(me, lax.rem(t + o, 4)), device_id_type=MESH)
    each_peer(lambda to: pl.semaphore_signal(barrier, inc=1, device_id=(to, t), device_id_type=MESH))

    cluster_row = cluster_ref[...]
    square = (rows, rows)
    i0, i1 = iota(square, 0), iota(square, 1)
    cluster_col = jnp.sum(jnp.where(i0 == i1, cluster_row, 0), axis=1, keepdims=True)
    slot_row = jnp.sum(
        jnp.where((cluster_col == cluster_row) & (i0 < i1), 1, 0), axis=0, keepdims=True)
    flat_row = (cluster_row // 2) * side + (cluster_row % 2) * bucket + slot_row
    place[...] = jnp.where(iota(place.shape, 0) == flat_row, 1.0, 0.0).astype(BF16)

    def project(i):
        span = pl.ds(i * half, half)
        xs = x_v[span, :]
        gained = xs * gain_ref[...].reshape(1, width)
        values[span, :] = jnp.dot(gained, vw_v[...], preferred_element_type=F32).astype(BF16)

    load_x(0).wait()
    load_vw.wait()
    load_ow(chunk, part - chunk, in_sem.at[4])
    project(0)
    load_x(1).wait()
    project(1)
    drain(ow_v.at[:, pl.ds(0, 4 * chunk)], in_sem.at[3])
    pl.semaphore_wait(barrier, 3 + owners - 1)

    def copy_a(k):
        return pltpu.make_async_remote_copy(
            send_a.at[k], recv_a.at[k], a_s.at[k], a_r.at[k], device_id=(me, partner), device_id_type=MESH)

    def copy_b(k):
        return pltpu.make_async_remote_copy(
            send_b.at[k], recv_b.at[k], b_s.at[k], b_r.at[k], device_id=(me, across), device_id_type=MESH)

    def start_c(k, h):
        each_peer(lambda to: pltpu.make_async_remote_copy(
            send_c.at[k, to, h], recv_c.at[k, h, me], c_s.at[k, h], c_r.at[k, h],
            device_id=(to, t), device_id_type=MESH).start())
        recv_c[k, h, me] = send_c[k, me, h]

    def term(quarter, k):
        columns = pl.ds(pl.multiple_of(quarter * part + k * chunk, chunk), chunk)
        w = ow_v[:, columns].astype(F32)
        kv_local = values.shape[1] // HEAD_DIM
        w = w.reshape(kv_local, HEADS // KV_HEADS, HEAD_DIM, chunk)
        w = jnp.sum(w, axis=1).reshape(kv_local * HEAD_DIM, chunk).astype(BF16)
        return jnp.dot(values[...], w, preferred_element_type=F32).astype(BF16)

    def stage_a(k):
        for h in range(2):
            send_a[k, h] = term(2 * h + 1 - core, k)
        copy_a(k).start()
        for h in range(2):
            keep_a[k, h] = term(2 * h + core, k)

    def stage_b(k):
        copy_a(k).wait_recv()
        send_b[k] = (keep_a[k, 1 - xh].astype(F32) + recv_a[k, 1 - xh].astype(F32)).astype(BF16)
        copy_b(k).start()

    def stage_c(k):
        copy_b(k).wait_recv()
        columns = pl.ds(pl.multiple_of(t * part + k * chunk, chunk), chunk)
        attention = keep_a[k, xh].astype(F32) + recv_a[k, xh].astype(F32) + recv_b[k].astype(F32)
        hidden = (x_v[:, columns].astype(F32) + attention * scale_v[...]).astype(BF16)
        placed = jnp.dot(place[...], hidden, preferred_element_type=F32).astype(BF16)
        send_c[k] = placed.reshape(owners, 2, side, chunk)
        start_c(k, 1 - xh)

        @pl.when(k % 2 == 0)
        def _():
            start_c(k // 2, xh)

    def step(s, _):
        @pl.when(s == 1)
        def _():
            drain(ow_v.at[:, pl.ds(0, 4 * (part - chunk))], in_sem.at[4])

        @pl.when(s < chunks)
        def _():
            stage_a(s)

        @pl.when((s > 0) & (s <= chunks))
        def _():
            stage_b(s - 1)

        @pl.when(s >= LAG)
        def _():
            stage_c(s - LAG)

        return 0

    lax.fori_loop(0, 2, step, 0)

    def row_scale(i, _):
        span = pl.ds(pl.multiple_of(i * 128, 128), 128)
        xs = x_v[span, :].astype(F32)
        scale_v[span, :] = lax.rsqrt(jnp.sum(xs * xs, axis=1, keepdims=True) * (1.0 / width) + 1e-05)
        return 0

    lax.fori_loop(0, rows // 128, row_scale, 0)
    rank = priority_ref[...]
    high, low = (rank // 128).astype(F32), (rank % 128).astype(F32)
    line = iota((8, rows), 0)
    meta = jnp.where(line == 0, high, jnp.where(line == 1, low, jnp.where(line == 2, 1.0, 0.0)))
    meta = meta.astype(BF16)

    def rank_block(to, _):
        s = iota((128, rows), 0)
        hit = (s + to * per_owner == flat_row) & (s < per_owner)
        got = lax.dot_general(
            meta, jnp.where(hit, 1.0, 0.0).astype(BF16), (((1,), (1,)), ((), ())),
            preferred_element_type=F32)
        line = got[0:1] * 128.0 + got[1:2] + (1.0 - got[2:3]) * float(sentinel)
        send_r[to] = jnp.broadcast_to(line, (8, 128))
        return 0

    lax.fori_loop(0, owners, rank_block, 0)
    recv_r[me] = send_r[me]
    each_peer(lambda to: pltpu.make_async_remote_copy(
        send_r.at[to], recv_r.at[me], r_s, r_r, device_id=(to, t), device_id_type=MESH).start())

    lax.fori_loop(2, chunks + LAG, step, 0)
    lax.fori_loop(chunks // 2, chunks - HELD, lambda k, _: start_c(k, xh) or 0, 0)
    others = pl.ds(0, owners - 1)
    gram[...] = jnp.zeros_like(gram)

    def stage_d(h):
        def one(k, _):
            drain(recv_c.at[k, h, others], c_r.at[k, h])
            for c in range(2):
                if bucket % 16 == 0:
                    members = recv_c[k, h, :, c * bucket:(c + 1) * bucket, :].reshape(capacity, chunk)
                else:
                    every = recv_c[k, h].reshape(owners * side, chunk)
                    shape = (capacity, owners * side)
                    r = iota(shape, 0)
                    pick = (r // bucket) * side + c * bucket + r % bucket == iota(shape, 1)
                    members = jnp.dot(
                        jnp.where(pick, 1.0, 0.0).astype(BF16), every, preferred_element_type=F32)
                    members = members.astype(BF16)
                gram[2 * h + c] += lax.dot_general(
                    members, members, (((1,), (1,)), ((), ())), preferred_element_type=F32)
            return 0

        lax.fori_loop(0, chunks, one, 0)

    def copy_e(h):
        return pltpu.make_async_remote_copy(
            gram.at[2 * h + 1 - core], recv_e.at[h], e_s.at[h], e_r.at[h],
            device_id=(me, partner), device_id_type=MESH)

    copy_f = pltpu.make_async_remote_copy(
        send_f, recv_f, f_s, f_r, device_id=(me, across), device_id_type=MESH)

    stage_d(1 - xh)
    copy_e(1 - xh).start()
    copy_e(1 - xh).wait_recv()
    send_f[...] = gram[2 * (1 - xh) + core] + recv_e[1 - xh]
    copy_f.start()
    lax.fori_loop(chunks - HELD, chunks, lambda k, _: start_c(k, xh) or 0, 0)

    drain(recv_r.at[others], r_r)
    ranks = recv_r[:, 0, :]
    r = iota((capacity, owners), 0)
    expand = jnp.where(r // bucket == iota((capacity, owners), 1), 1.0, 0.0)
    spread = jnp.dot(expand, ranks, precision=lax.Precision.HIGHEST, preferred_element_type=F32)
    r = iota((capacity, 128), 0)
    lane = xh * side + core * bucket + r % bucket
    rank_col = jnp.sum(
        jnp.where(iota((capacity, 128), 1) == lane, spread, 0.0), axis=1, keepdims=True)
    eye = iota((capacity, capacity), 0) == iota((capacity, capacity), 1)
    rank_row = jnp.sum(jnp.where(eye, rank_col, 0.0), axis=0, keepdims=True)
    spot = me * bucket + slot_row
    pick = jnp.where(iota((128, rows), 0) == spot % 128, 1.0, 0.0)

    stage_d(xh)
    copy_e(xh).start()
    copy_f.wait_recv()
    copy_e(xh).wait_recv()
    total = gram[2 * xh + core] + recv_e[xh] + recv_f[...]
    diagonal = jnp.where(eye, total, 0.0)
    norm_row = lax.rsqrt(jnp.sum(diagonal, axis=0, keepdims=True) + 1e-06)
    norm_col = lax.rsqrt(jnp.sum(diagonal, axis=1, keepdims=True) + 1e-06)
    similarity = total * norm_col * norm_row
    highest = jnp.max(jnp.where(rank_col < rank_row, similarity, -2.0), axis=0, keepdims=True)
    highest = jnp.maximum(highest, -1.0)
    best_t[t] = jnp.broadcast_to(highest, (8, capacity))

    def copy_g(to, frm):
        return pltpu.make_async_remote_copy(
            best_t.at[frm], best_t.at[frm], g_s.at[to], g_r.at[frm], device_id=(me, to), device_id_type=MESH)

    for o in range(1, 4):
        copy_g(lax.rem(t + o, 4), t).start()
    for o in range(1, 4):
        copy_g(t, lax.rem(t + o, 4)).wait_recv()
    line = iota((8, 128), 0)
    rows_h = jnp.zeros((8, 128), F32)
    for c in range(CLU_DEV):
        for j in range(2):
            rows_h = jnp.where(line == j * CLU_DEV + c, best_t[c, :, j * 128:(j + 1) * 128], rows_h)
    send_h[...] = rows_h
    each_peer(lambda to: pltpu.make_async_remote_copy(
        send_h, recv_h.at[me], h_s, h_r, device_id=(to, t), device_id_type=MESH).start())
    recv_h[me] = rows_h
    drain(recv_h.at[others], h_r)
    returned = recv_h[...].reshape(owners * 8, 128)
    found = jnp.dot(returned, pick, precision=lax.Precision.HIGHEST, preferred_element_type=F32)
    where = (cluster_row // CLU_DEV) * 8 + (spot // 128) * CLU_DEV + cluster_row % CLU_DEV
    out_ref[...] = jnp.sum(
        jnp.where(iota((owners * 8, rows), 0) == where, found, 0.0), axis=0, keepdims=True)

    def sent_k(k, _):
        copy_a(k).wait_send()
        copy_b(k).wait_send()
        for h in range(2):
            drain(recv_c.at[k, h, others], c_s.at[k, h])
        return 0

    lax.fori_loop(0, chunks, sent_k, 0)
    drain(recv_r.at[others], r_s)
    drain(recv_h.at[others], h_s)
    copy_e(1 - xh).wait_send()
    copy_e(xh).wait_send()
    copy_f.wait_send()
    for o in range(1, 4):
        copy_g(lax.rem(t + o, 4), t).wait_send()


def shards(final_input, norm_gain, value_weight, out_weight, cluster, priority):
    rows, width = final_input.shape
    owners = lax.axis_size("dp")
    tensor = lax.axis_size("tensor")
    part = width // tensor
    chunk = part // CHUNKS
    bucket = max(2, 2 * rows // (CLU_DEV * owners))
    side = max(16, 2 * bucket)
    per_owner = 2 * side
    capacity = owners * bucket
    kv = value_weight.shape[1]
    vmem = pl.BlockSpec(memory_space=pltpu.VMEM)
    anywhere = pl.BlockSpec(memory_space=pl.ANY)
    dma = pltpu.SemaphoreType.DMA
    best = pl.pallas_call(
        functools.partial(kernel, owners, bucket),
        out_shape=jax.ShapeDtypeStruct((1, rows), F32),
        in_specs=[anywhere, vmem, anywhere, anywhere, vmem, vmem],
        out_specs=vmem,
        scratch_shapes=[
            pltpu.VMEM((rows, width), BF16),
            pltpu.VMEM((width, kv), BF16),
            pltpu.VMEM(out_weight.shape, BF16),
            pltpu.VMEM((rows, 1), F32),
            pltpu.VMEM((rows, kv), BF16),
            pltpu.VMEM((CHUNKS, 2, rows, chunk), BF16),
            pltpu.VMEM((CHUNKS, 2, rows, chunk), BF16),
            pltpu.VMEM((CHUNKS, 2, rows, chunk), BF16),
            pltpu.VMEM((CHUNKS, rows, chunk), BF16),
            pltpu.VMEM((CHUNKS, rows, chunk), BF16),
            pltpu.VMEM((owners * per_owner, rows), BF16),
            pltpu.VMEM((CHUNKS, owners, 2, side, chunk), BF16),
            pltpu.VMEM((CHUNKS, 2, owners, side, chunk), BF16),
            pltpu.VMEM((owners, 8, 128), F32),
            pltpu.VMEM((owners, 8, 128), F32),
            pltpu.VMEM((CLU_DEV, capacity, capacity), F32),
            pltpu.VMEM((2, capacity, capacity), F32),
            pltpu.VMEM((capacity, capacity), F32),
            pltpu.VMEM((capacity, capacity), F32),
            pltpu.VMEM((CLU_DEV, 8, capacity), F32),
            pltpu.VMEM((8, 128), F32),
            pltpu.VMEM((owners, 8, 128), F32),
            dma((5,)),
            dma((CHUNKS,)), dma((CHUNKS,)),
            dma((CHUNKS,)), dma((CHUNKS,)),
            dma((CHUNKS, 2)), dma((CHUNKS, 2)),
            dma, dma,
            dma((2,)), dma((2,)),
            dma, dma,
            dma((4,)), dma((4,)),
            dma, dma,
        ],
        compiler_params=pltpu.CompilerParams(
            collective_id=0, has_side_effects=True, vmem_limit_bytes=56 * 1024 * 1024),
        cost_estimate=pl.CostEstimate(flops=6_000_000_000, bytes_accessed=16_000_000, transcendentals=0),
    )(final_input, norm_gain, value_weight, out_weight, cluster.reshape(1, rows), priority.reshape(1, rows))
    return best.reshape(rows)


def solution(mesh):
    in_specs = (P("dp", None), P(), P(None, "tensor"), P("tensor", None), P("dp", None), P("dp"))
    out_specs = P("dp")
    return jax.shard_map(shards, mesh=mesh, in_specs=in_specs, out_specs=out_specs, check_vma=False)
```

```python
import functools

import jax
import jax.numpy as jnp
from jax import lax
from jax.experimental import pallas as pl
from jax.experimental.pallas import tpu as pltpu
from jax.sharding import PartitionSpec as P

HEADS = 32
KV_HEADS = 8
HEAD_DIM = 128
CLU_DEV = 4
CHUNKS = 8
LAG = 2
HELD = 2
MESH = pl.DeviceIdType.MESH
BF16 = jnp.bfloat16
F32 = jnp.float32
I32 = jnp.int32


def iota(shape, dim):
    return lax.broadcasted_iota(I32, shape, dim)


def drain(ref, sem):
    pltpu.make_async_copy(ref, ref, sem).wait()


def kernel(
    owners, bucket,
    x_hbm, gain_ref, vw_hbm, ow_hbm, cluster_ref, priority_ref, out_ref,
    x_v, vw_v, ow_v, scale_v, values, send_a, keep_a, recv_a, send_b, recv_b,
    place, send_c, recv_c, send_r, recv_r, gram, recv_e, send_f, recv_f, best_t, send_h, recv_h,
    in_sem, a_s, a_r, b_s, b_r, c_s, c_r, r_s, r_r, e_s, e_r, f_s, f_r, g_s, g_r, h_s, h_r,
):
    rows, width = x_v.shape
    chunks, _, chunk = recv_b.shape
    part = chunk * chunks
    side = recv_c.shape[3]
    per_owner = 2 * side
    capacity = owners * bucket
    sentinel = owners * rows
    me = lax.axis_index("dp")
    t = lax.axis_index("tensor")
    xh, core = t // 2, t % 2
    partner = 2 * xh + (1 - core)
    across = 2 * (1 - xh) + core
    half = rows // 2

    def peer(o):
        found, bit = 0, 1
        while bit < owners:
            found = found + lax.rem(me // bit + o // bit, 2) * bit
            bit = 2 * bit
        return found

    def each_peer(act):
        def step(i, _):
            act(peer(owners - 1 - i // 2 - lax.rem(i, 2) * (owners // 2)))
            return 0

        lax.fori_loop(0, owners - 1, step, 0)

    def load_x(i):
        span = pl.ds(i * half, half)
        return pltpu.make_async_copy(x_hbm.at[span], x_v.at[span], in_sem.at[i])

    load_vw = pltpu.make_async_copy(vw_hbm, vw_v, in_sem.at[2])

    def load_ow(start, size, sem):
        for q in range(4):
            span = pl.ds(q * part + start, size)
            pltpu.make_async_copy(ow_hbm.at[:, span], ow_v.at[:, span], sem).start()

    load_x(0).start()
    load_vw.start()
    load_x(1).start()
    load_ow(0, chunk, in_sem.at[3])

    barrier = pltpu.get_barrier_semaphore()
    for o in range(1, 4):
        pl.semaphore_signal(barrier, inc=1, device_id=(me, lax.rem(t + o, 4)), device_id_type=MESH)
    each_peer(lambda to: pl.semaphore_signal(barrier, inc=1, device_id=(to, t), device_id_type=MESH))

    cluster_row = cluster_ref[...]
    square = (rows, rows)
    i0, i1 = iota(square, 0), iota(square, 1)
    cluster_col = jnp.sum(jnp.where(i0 == i1, cluster_row, 0), axis=1, keepdims=True)
    slot_row = jnp.sum(
        jnp.where((cluster_col == cluster_row) & (i0 < i1), 1, 0), axis=0, keepdims=True)
    flat_row = (cluster_row // 2) * side + (cluster_row % 2) * bucket + slot_row
    place[...] = jnp.where(iota(place.shape, 0) == flat_row, 1.0, 0.0).astype(BF16)

    def project(i):
        span = pl.ds(i * half, half)
        xs = x_v[span, :]
        gained = xs * gain_ref[...].reshape(1, width)
        values[span, :] = jnp.dot(gained, vw_v[...], preferred_element_type=F32).astype(BF16)

    load_x(0).wait()
    load_vw.wait()
    load_ow(chunk, part - chunk, in_sem.at[4])
    project(0)
    load_x(1).wait()
    project(1)
    drain(ow_v.at[:, pl.ds(0, 4 * chunk)], in_sem.at[3])
    pl.semaphore_wait(barrier, 3 + owners - 1)

    def copy_a(k):
        return pltpu.make_async_remote_copy(
            send_a.at[k], recv_a.at[k], a_s.at[k], a_r.at[k], device_id=(me, partner), device_id_type=MESH)

    def copy_b(k):
        return pltpu.make_async_remote_copy(
            send_b.at[k], recv_b.at[k], b_s.at[k], b_r.at[k], device_id=(me, across), device_id_type=MESH)

    def start_c(k, h):
        each_peer(lambda to: pltpu.make_async_remote_copy(
            send_c.at[k, to, h], recv_c.at[k, h, me], c_s.at[k, h], c_r.at[k, h],
            device_id=(to, t), device_id_type=MESH).start())
        recv_c[k, h, me] = send_c[k, me, h]

    def term(quarter, k):
        columns = pl.ds(pl.multiple_of(quarter * part + k * chunk, chunk), chunk)
        w = ow_v[:, columns].astype(F32)
        kv_local = values.shape[1] // HEAD_DIM
        w = w.reshape(kv_local, HEADS // KV_HEADS, HEAD_DIM, chunk)
        w = jnp.sum(w, axis=1).reshape(kv_local * HEAD_DIM, chunk).astype(BF16)
        return jnp.dot(values[...], w, preferred_element_type=F32).astype(BF16)

    def stage_a(k):
        for h in range(2):
            send_a[k, h] = term(2 * h + 1 - core, k)
        copy_a(k).start()
        for h in range(2):
            keep_a[k, h] = term(2 * h + core, k)

    def stage_b(k):
        copy_a(k).wait_recv()
        send_b[k] = (keep_a[k, 1 - xh].astype(F32) + recv_a[k, 1 - xh].astype(F32)).astype(BF16)
        copy_b(k).start()

    def stage_c(k):
        copy_b(k).wait_recv()
        columns = pl.ds(pl.multiple_of(t * part + k * chunk, chunk), chunk)
        attention = keep_a[k, xh].astype(F32) + recv_a[k, xh].astype(F32) + recv_b[k].astype(F32)
        hidden = (x_v[:, columns].astype(F32) + attention * scale_v[...]).astype(BF16)
        placed = jnp.dot(place[...], hidden, preferred_element_type=F32).astype(BF16)
        send_c[k] = placed.reshape(owners, 2, side, chunk)
        start_c(k, 1 - xh)

        @pl.when(k % 2 == 0)
        def _():
            start_c(k // 2, xh)

    def step(s, _):
        @pl.when(s == 1)
        def _():
            drain(ow_v.at[:, pl.ds(0, 4 * (part - chunk))], in_sem.at[4])

        @pl.when(s < chunks)
        def _():
            stage_a(s)

        @pl.when((s > 0) & (s <= chunks))
        def _():
            stage_b(s - 1)

        @pl.when(s >= LAG)
        def _():
            stage_c(s - LAG)

        return 0

    lax.fori_loop(0, 2, step, 0)

    def row_scale(i, _):
        span = pl.ds(pl.multiple_of(i * 128, 128), 128)
        xs = x_v[span, :].astype(F32)
        scale_v[span, :] = lax.rsqrt(jnp.sum(xs * xs, axis=1, keepdims=True) * (1.0 / width) + 1e-05)
        return 0

    lax.fori_loop(0, rows // 128, row_scale, 0)
    rank = priority_ref[...]
    high, low = (rank // 128).astype(F32), (rank % 128).astype(F32)
    line = iota((8, rows), 0)
    meta = jnp.where(line == 0, high, jnp.where(line == 1, low, jnp.where(line == 2, 1.0, 0.0)))
    meta = meta.astype(BF16)

    def rank_block(to, _):
        s = iota((128, rows), 0)
        hit = (s + to * per_owner == flat_row) & (s < per_owner)
        got = lax.dot_general(
            meta, jnp.where(hit, 1.0, 0.0).astype(BF16), (((1,), (1,)), ((), ())),
            preferred_element_type=F32)
        line = got[0:1] * 128.0 + got[1:2] + (1.0 - got[2:3]) * float(sentinel)
        send_r[to] = jnp.broadcast_to(line, (8, 128))
        return 0

    lax.fori_loop(0, owners, rank_block, 0)
    recv_r[me] = send_r[me]
    each_peer(lambda to: pltpu.make_async_remote_copy(
        send_r.at[to], recv_r.at[me], r_s, r_r, device_id=(to, t), device_id_type=MESH).start())

    lax.fori_loop(2, chunks + LAG, step, 0)
    lax.fori_loop(chunks // 2, chunks - HELD, lambda k, _: start_c(k, xh) or 0, 0)
    others = pl.ds(0, owners - 1)
    gram[...] = jnp.zeros_like(gram)

    def stage_d(h):
        def one(k, _):
            drain(recv_c.at[k, h, others], c_r.at[k, h])
            for c in range(2):
                if bucket % 16 == 0:
                    members = recv_c[k, h, :, c * bucket:(c + 1) * bucket, :].reshape(capacity, chunk)
                else:
                    every = recv_c[k, h].reshape(owners * side, chunk)
                    shape = (capacity, owners * side)
                    r = iota(shape, 0)
                    pick = (r // bucket) * side + c * bucket + r % bucket == iota(shape, 1)
                    members = jnp.dot(
                        jnp.where(pick, 1.0, 0.0).astype(BF16), every, preferred_element_type=F32)
                    members = members.astype(BF16)
                gram[2 * h + c] += lax.dot_general(
                    members, members, (((1,), (1,)), ((), ())), preferred_element_type=F32)
            return 0

        lax.fori_loop(0, chunks, one, 0)

    def copy_e(h):
        return pltpu.make_async_remote_copy(
            gram.at[2 * h + 1 - core], recv_e.at[h], e_s.at[h], e_r.at[h],
            device_id=(me, partner), device_id_type=MESH)

    copy_f = pltpu.make_async_remote_copy(
        send_f, recv_f, f_s, f_r, device_id=(me, across), device_id_type=MESH)

    stage_d(1 - xh)
    copy_e(1 - xh).start()
    copy_e(1 - xh).wait_recv()
    send_f[...] = gram[2 * (1 - xh) + core] + recv_e[1 - xh]
    copy_f.start()
    lax.fori_loop(chunks - HELD, chunks, lambda k, _: start_c(k, xh) or 0, 0)

    drain(recv_r.at[others], r_r)
    ranks = recv_r[:, 0, :]
    r = iota((capacity, owners), 0)
    expand = jnp.where(r // bucket == iota((capacity, owners), 1), 1.0, 0.0)
    spread = jnp.dot(expand, ranks, precision=lax.Precision.HIGHEST, preferred_element_type=F32)
    r = iota((capacity, 128), 0)
    lane = xh * side + core * bucket + r % bucket
    rank_col = jnp.sum(
        jnp.where(iota((capacity, 128), 1) == lane, spread, 0.0), axis=1, keepdims=True)
    eye = iota((capacity, capacity), 0) == iota((capacity, capacity), 1)
    rank_row = jnp.sum(jnp.where(eye, rank_col, 0.0), axis=0, keepdims=True)
    spot = me * bucket + slot_row
    pick = jnp.where(iota((128, rows), 0) == spot % 128, 1.0, 0.0)

    stage_d(xh)
    copy_e(xh).start()
    copy_f.wait_recv()
    copy_e(xh).wait_recv()
    total = gram[2 * xh + core] + recv_e[xh] + recv_f[...]
    diagonal = jnp.where(eye, total, 0.0)
    norm_row = lax.rsqrt(jnp.sum(diagonal, axis=0, keepdims=True) + 1e-06)
    norm_col = lax.rsqrt(jnp.sum(diagonal, axis=1, keepdims=True) + 1e-06)
    similarity = total * norm_col * norm_row
    highest = jnp.max(jnp.where(rank_col < rank_row, similarity, -2.0), axis=0, keepdims=True)
    highest = jnp.maximum(highest, -1.0)
    best_t[t] = jnp.broadcast_to(highest, (8, capacity))

    def copy_g(to, frm):
        return pltpu.make_async_remote_copy(
            best_t.at[frm], best_t.at[frm], g_s.at[to], g_r.at[frm], device_id=(me, to), device_id_type=MESH)

    for o in range(1, 4):
        copy_g(lax.rem(t + o, 4), t).start()
    for o in range(1, 4):
        copy_g(t, lax.rem(t + o, 4)).wait_recv()
    line = iota((8, 128), 0)
    rows_h = jnp.zeros((8, 128), F32)
    for c in range(CLU_DEV):
        for j in range(2):
            rows_h = jnp.where(line == j * CLU_DEV + c, best_t[c, :, j * 128:(j + 1) * 128], rows_h)
    send_h[...] = rows_h
    each_peer(lambda to: pltpu.make_async_remote_copy(
        send_h, recv_h.at[me], h_s, h_r, device_id=(to, t), device_id_type=MESH).start())
    recv_h[me] = rows_h
    drain(recv_h.at[others], h_r)
    returned = recv_h[...].reshape(owners * 8, 128)
    found = jnp.dot(returned, pick, precision=lax.Precision.HIGHEST, preferred_element_type=F32)
    where = (cluster_row // CLU_DEV) * 8 + (spot // 128) * CLU_DEV + cluster_row % CLU_DEV
    out_ref[...] = jnp.sum(
        jnp.where(iota((owners * 8, rows), 0) == where, found, 0.0), axis=0, keepdims=True)

    def sent_k(k, _):
        copy_a(k).wait_send()
        copy_b(k).wait_send()
        for h in range(2):
            drain(recv_c.at[k, h, others], c_s.at[k, h])
        return 0

    lax.fori_loop(0, chunks, sent_k, 0)
    drain(recv_r.at[others], r_s)
    drain(recv_h.at[others], h_s)
    copy_e(1 - xh).wait_send()
    copy_e(xh).wait_send()
    copy_f.wait_send()
    for o in range(1, 4):
        copy_g(lax.rem(t + o, 4), t).wait_send()


def shards(final_input, norm_gain, value_weight, out_weight, cluster, priority):
    rows, width = final_input.shape
    owners = lax.axis_size("dp")
    tensor = lax.axis_size("tensor")
    part = width // tensor
    chunk = part // CHUNKS
    bucket = max(2, 2 * rows // (CLU_DEV * owners))
    side = max(16, 2 * bucket)
    per_owner = 2 * side
    capacity = owners * bucket
    kv = value_weight.shape[1]
    vmem = pl.BlockSpec(memory_space=pltpu.VMEM)
    anywhere = pl.BlockSpec(memory_space=pl.ANY)
    dma = pltpu.SemaphoreType.DMA
    best = pl.pallas_call(
        functools.partial(kernel, owners, bucket),
        out_shape=jax.ShapeDtypeStruct((1, rows), F32),
        in_specs=[anywhere, vmem, anywhere, anywhere, vmem, vmem],
        out_specs=vmem,
        scratch_shapes=[
            pltpu.VMEM((rows, width), BF16),
            pltpu.VMEM((width, kv), BF16),
            pltpu.VMEM(out_weight.shape, BF16),
            pltpu.VMEM((rows, 1), F32),
            pltpu.VMEM((rows, kv), BF16),
            pltpu.VMEM((CHUNKS, 2, rows, chunk), BF16),
            pltpu.VMEM((CHUNKS, 2, rows, chunk), BF16),
            pltpu.VMEM((CHUNKS, 2, rows, chunk), BF16),
            pltpu.VMEM((CHUNKS, rows, chunk), BF16),
            pltpu.VMEM((CHUNKS, rows, chunk), BF16),
            pltpu.VMEM((owners * per_owner, rows), BF16),
            pltpu.VMEM((CHUNKS, owners, 2, side, chunk), BF16),
            pltpu.VMEM((CHUNKS, 2, owners, side, chunk), BF16),
            pltpu.VMEM((owners, 8, 128), F32),
            pltpu.VMEM((owners, 8, 128), F32),
            pltpu.VMEM((CLU_DEV, capacity, capacity), F32),
            pltpu.VMEM((2, capacity, capacity), F32),
            pltpu.VMEM((capacity, capacity), F32),
            pltpu.VMEM((capacity, capacity), F32),
            pltpu.VMEM((CLU_DEV, 8, capacity), F32),
            pltpu.VMEM((8, 128), F32),
            pltpu.VMEM((owners, 8, 128), F32),
            dma((5,)),
            dma((CHUNKS,)), dma((CHUNKS,)),
            dma((CHUNKS,)), dma((CHUNKS,)),
            dma((CHUNKS, 2)), dma((CHUNKS, 2)),
            dma, dma,
            dma((2,)), dma((2,)),
            dma, dma,
            dma((4,)), dma((4,)),
            dma, dma,
        ],
        compiler_params=pltpu.CompilerParams(
            collective_id=0, has_side_effects=True, vmem_limit_bytes=56 * 1024 * 1024),
        cost_estimate=pl.CostEstimate(flops=6_000_000_000, bytes_accessed=16_000_000, transcendentals=0),
    )(final_input, norm_gain, value_weight, out_weight, cluster.reshape(1, rows), priority.reshape(1, rows))
    return best.reshape(rows)


def solution(mesh):
    in_specs = (P("dp", None), P(), P(None, "tensor"), P("tensor", None), P("dp", None), P("dp"))
    out_specs = P("dp")
    return jax.shard_map(shards, mesh=mesh, in_specs=in_specs, out_specs=out_specs, check_vma=False)
```

```python
import functools

import jax
import jax.numpy as jnp
from jax import lax
from jax.experimental import pallas as pl
from jax.experimental.pallas import tpu as pltpu
from jax.sharding import PartitionSpec as P

HEADS = 32
KV_HEADS = 8
HEAD_DIM = 128
CLU_DEV = 4
CHUNKS = 8
LAG = 2
HELD = 3
MESH = pl.DeviceIdType.MESH
BF16 = jnp.bfloat16
F32 = jnp.float32
I32 = jnp.int32


def iota(shape, dim):
    return lax.broadcasted_iota(I32, shape, dim)


def drain(ref, sem):
    pltpu.make_async_copy(ref, ref, sem).wait()


def kernel(
    owners, bucket,
    x_hbm, gain_ref, vw_hbm, ow_hbm, cluster_ref, priority_ref, out_ref,
    x_v, vw_v, ow_v, scale_v, values, send_a, keep_a, recv_a, send_b, recv_b,
    place, send_c, recv_c, send_r, recv_r, gram, recv_e, send_f, recv_f, best_t, send_h, recv_h,
    in_sem, a_s, a_r, b_s, b_r, c_s, c_r, r_s, r_r, e_s, e_r, f_s, f_r, g_s, g_r, h_s, h_r,
):
    rows, width = x_v.shape
    chunks, _, chunk = recv_b.shape
    part = chunk * chunks
    side = recv_c.shape[3]
    per_owner = 2 * side
    capacity = owners * bucket
    sentinel = owners * rows
    me = lax.axis_index("dp")
    t = lax.axis_index("tensor")
    xh, core = t // 2, t % 2
    partner = 2 * xh + (1 - core)
    across = 2 * (1 - xh) + core
    half = rows // 2

    def peer(o):
        found, bit = 0, 1
        while bit < owners:
            found = found + lax.rem(me // bit + o // bit, 2) * bit
            bit = 2 * bit
        return found

    def each_peer(act):
        def step(i, _):
            act(peer(owners - 1 - i // 2 - lax.rem(i, 2) * (owners // 2)))
            return 0

        lax.fori_loop(0, owners - 1, step, 0)

    def load_x(i):
        span = pl.ds(i * half, half)
        return pltpu.make_async_copy(x_hbm.at[span], x_v.at[span], in_sem.at[i])

    load_vw = pltpu.make_async_copy(vw_hbm, vw_v, in_sem.at[2])

    def load_ow(start, size, sem):
        for q in range(4):
            span = pl.ds(q * part + start, size)
            pltpu.make_async_copy(ow_hbm.at[:, span], ow_v.at[:, span], sem).start()

    load_x(0).start()
    load_vw.start()
    load_x(1).start()
    load_ow(0, chunk, in_sem.at[3])

    barrier = pltpu.get_barrier_semaphore()
    for o in range(1, 4):
        pl.semaphore_signal(barrier, inc=1, device_id=(me, lax.rem(t + o, 4)), device_id_type=MESH)
    each_peer(lambda to: pl.semaphore_signal(barrier, inc=1, device_id=(to, t), device_id_type=MESH))

    cluster_row = cluster_ref[...]
    square = (rows, rows)
    i0, i1 = iota(square, 0), iota(square, 1)
    cluster_col = jnp.sum(jnp.where(i0 == i1, cluster_row, 0), axis=1, keepdims=True)
    slot_row = jnp.sum(
        jnp.where((cluster_col == cluster_row) & (i0 < i1), 1, 0), axis=0, keepdims=True)
    flat_row = (cluster_row // 2) * side + (cluster_row % 2) * bucket + slot_row
    place[...] = jnp.where(iota(place.shape, 0) == flat_row, 1.0, 0.0).astype(BF16)

    def project(i):
        span = pl.ds(i * half, half)
        xs = x_v[span, :]
        gained = xs * gain_ref[...].reshape(1, width)
        values[span, :] = jnp.dot(gained, vw_v[...], preferred_element_type=F32).astype(BF16)

    load_x(0).wait()
    load_vw.wait()
    load_ow(chunk, part - chunk, in_sem.at[4])
    project(0)
    load_x(1).wait()
    project(1)
    drain(ow_v.at[:, pl.ds(0, 4 * chunk)], in_sem.at[3])
    pl.semaphore_wait(barrier, 3 + owners - 1)

    def copy_a(k):
        return pltpu.make_async_remote_copy(
            send_a.at[k], recv_a.at[k], a_s.at[k], a_r.at[k], device_id=(me, partner), device_id_type=MESH)

    def copy_b(k):
        return pltpu.make_async_remote_copy(
            send_b.at[k], recv_b.at[k], b_s.at[k], b_r.at[k], device_id=(me, across), device_id_type=MESH)

    def start_c(k, h):
        each_peer(lambda to: pltpu.make_async_remote_copy(
            send_c.at[k, to, h], recv_c.at[k, h, me], c_s.at[k, h], c_r.at[k, h],
            device_id=(to, t), device_id_type=MESH).start())
        recv_c[k, h, me] = send_c[k, me, h]

    def term(quarter, k):
        columns = pl.ds(pl.multiple_of(quarter * part + k * chunk, chunk), chunk)
        w = ow_v[:, columns].astype(F32)
        kv_local = values.shape[1] // HEAD_DIM
        w = w.reshape(kv_local, HEADS // KV_HEADS, HEAD_DIM, chunk)
        w = jnp.sum(w, axis=1).reshape(kv_local * HEAD_DIM, chunk).astype(BF16)
        return jnp.dot(values[...], w, preferred_element_type=F32).astype(BF16)

    def stage_a(k):
        for h in range(2):
            send_a[k, h] = term(2 * h + 1 - core, k)
        copy_a(k).start()
        for h in range(2):
            keep_a[k, h] = term(2 * h + core, k)

    def stage_b(k):
        copy_a(k).wait_recv()
        send_b[k] = (keep_a[k, 1 - xh].astype(F32) + recv_a[k, 1 - xh].astype(F32)).astype(BF16)
        copy_b(k).start()

    def stage_c(k):
        copy_b(k).wait_recv()
        columns = pl.ds(pl.multiple_of(t * part + k * chunk, chunk), chunk)
        attention = keep_a[k, xh].astype(F32) + recv_a[k, xh].astype(F32) + recv_b[k].astype(F32)
        hidden = (x_v[:, columns].astype(F32) + attention * scale_v[...]).astype(BF16)
        placed = jnp.dot(place[...], hidden, preferred_element_type=F32).astype(BF16)
        send_c[k] = placed.reshape(owners, 2, side, chunk)
        start_c(k, 1 - xh)

        @pl.when(k % 2 == 0)
        def _():
            start_c(k // 2, xh)

    def step(s, _):
        @pl.when(s == 1)
        def _():
            drain(ow_v.at[:, pl.ds(0, 4 * (part - chunk))], in_sem.at[4])

        @pl.when(s < chunks)
        def _():
            stage_a(s)

        @pl.when((s > 0) & (s <= chunks))
        def _():
            stage_b(s - 1)

        @pl.when(s >= LAG)
        def _():
            stage_c(s - LAG)

        return 0

    lax.fori_loop(0, 2, step, 0)

    def row_scale(i, _):
        span = pl.ds(pl.multiple_of(i * 128, 128), 128)
        xs = x_v[span, :].astype(F32)
        scale_v[span, :] = lax.rsqrt(jnp.sum(xs * xs, axis=1, keepdims=True) * (1.0 / width) + 1e-05)
        return 0

    lax.fori_loop(0, rows // 128, row_scale, 0)
    rank = priority_ref[...]
    high, low = (rank // 128).astype(F32), (rank % 128).astype(F32)
    line = iota((8, rows), 0)
    meta = jnp.where(line == 0, high, jnp.where(line == 1, low, jnp.where(line == 2, 1.0, 0.0)))
    meta = meta.astype(BF16)

    def rank_block(to, _):
        s = iota((128, rows), 0)
        hit = (s + to * per_owner == flat_row) & (s < per_owner)
        got = lax.dot_general(
            meta, jnp.where(hit, 1.0, 0.0).astype(BF16), (((1,), (1,)), ((), ())),
            preferred_element_type=F32)
        line = got[0:1] * 128.0 + got[1:2] + (1.0 - got[2:3]) * float(sentinel)
        send_r[to] = jnp.broadcast_to(line, (8, 128))
        return 0

    lax.fori_loop(0, owners, rank_block, 0)
    recv_r[me] = send_r[me]
    each_peer(lambda to: pltpu.make_async_remote_copy(
        send_r.at[to], recv_r.at[me], r_s, r_r, device_id=(to, t), device_id_type=MESH).start())

    lax.fori_loop(2, chunks + LAG, step, 0)
    lax.fori_loop(chunks // 2, chunks - HELD, lambda k, _: start_c(k, xh) or 0, 0)
    others = pl.ds(0, owners - 1)
    gram[...] = jnp.zeros_like(gram)

    def stage_d(h):
        def one(k, _):
            drain(recv_c.at[k, h, others], c_r.at[k, h])
            for c in range(2):
                if bucket % 16 == 0:
                    members = recv_c[k, h, :, c * bucket:(c + 1) * bucket, :].reshape(capacity, chunk)
                else:
                    every = recv_c[k, h].reshape(owners * side, chunk)
                    shape = (capacity, owners * side)
                    r = iota(shape, 0)
                    pick = (r // bucket) * side + c * bucket + r % bucket == iota(shape, 1)
                    members = jnp.dot(
                        jnp.where(pick, 1.0, 0.0).astype(BF16), every, preferred_element_type=F32)
                    members = members.astype(BF16)
                gram[2 * h + c] += lax.dot_general(
                    members, members, (((1,), (1,)), ((), ())), preferred_element_type=F32)
            return 0

        lax.fori_loop(0, chunks, one, 0)

    def copy_e(h):
        return pltpu.make_async_remote_copy(
            gram.at[2 * h + 1 - core], recv_e.at[h], e_s.at[h], e_r.at[h],
            device_id=(me, partner), device_id_type=MESH)

    copy_f = pltpu.make_async_remote_copy(
        send_f, recv_f, f_s, f_r, device_id=(me, across), device_id_type=MESH)

    stage_d(1 - xh)
    copy_e(1 - xh).start()
    copy_e(1 - xh).wait_recv()
    send_f[...] = gram[2 * (1 - xh) + core] + recv_e[1 - xh]
    copy_f.start()
    lax.fori_loop(chunks - HELD, chunks, lambda k, _: start_c(k, xh) or 0, 0)

    drain(recv_r.at[others], r_r)
    ranks = recv_r[:, 0, :]
    r = iota((capacity, owners), 0)
    expand = jnp.where(r // bucket == iota((capacity, owners), 1), 1.0, 0.0)
    spread = jnp.dot(expand, ranks, precision=lax.Precision.HIGHEST, preferred_element_type=F32)
    r = iota((capacity, 128), 0)
    lane = xh * side + core * bucket + r % bucket
    rank_col = jnp.sum(
        jnp.where(iota((capacity, 128), 1) == lane, spread, 0.0), axis=1, keepdims=True)
    eye = iota((capacity, capacity), 0) == iota((capacity, capacity), 1)
    rank_row = jnp.sum(jnp.where(eye, rank_col, 0.0), axis=0, keepdims=True)
    spot = me * bucket + slot_row
    pick = jnp.where(iota((128, rows), 0) == spot % 128, 1.0, 0.0)

    stage_d(xh)
    copy_e(xh).start()
    copy_f.wait_recv()
    copy_e(xh).wait_recv()
    total = gram[2 * xh + core] + recv_e[xh] + recv_f[...]
    diagonal = jnp.where(eye, total, 0.0)
    norm_row = lax.rsqrt(jnp.sum(diagonal, axis=0, keepdims=True) + 1e-06)
    norm_col = lax.rsqrt(jnp.sum(diagonal, axis=1, keepdims=True) + 1e-06)
    similarity = total * norm_col * norm_row
    highest = jnp.max(jnp.where(rank_col < rank_row, similarity, -2.0), axis=0, keepdims=True)
    highest = jnp.maximum(highest, -1.0)
    best_t[t] = jnp.broadcast_to(highest, (8, capacity))

    def copy_g(to, frm):
        return pltpu.make_async_remote_copy(
            best_t.at[frm], best_t.at[frm], g_s.at[to], g_r.at[frm], device_id=(me, to), device_id_type=MESH)

    for o in range(1, 4):
        copy_g(lax.rem(t + o, 4), t).start()
    for o in range(1, 4):
        copy_g(t, lax.rem(t + o, 4)).wait_recv()
    line = iota((8, 128), 0)
    rows_h = jnp.zeros((8, 128), F32)
    for c in range(CLU_DEV):
        for j in range(2):
            rows_h = jnp.where(line == j * CLU_DEV + c, best_t[c, :, j * 128:(j + 1) * 128], rows_h)
    send_h[...] = rows_h
    each_peer(lambda to: pltpu.make_async_remote_copy(
        send_h, recv_h.at[me], h_s, h_r, device_id=(to, t), device_id_type=MESH).start())
    recv_h[me] = rows_h
    drain(recv_h.at[others], h_r)
    returned = recv_h[...].reshape(owners * 8, 128)
    found = jnp.dot(returned, pick, precision=lax.Precision.HIGHEST, preferred_element_type=F32)
    where = (cluster_row // CLU_DEV) * 8 + (spot // 128) * CLU_DEV + cluster_row % CLU_DEV
    out_ref[...] = jnp.sum(
        jnp.where(iota((owners * 8, rows), 0) == where, found, 0.0), axis=0, keepdims=True)

    def sent_k(k, _):
        copy_a(k).wait_send()
        copy_b(k).wait_send()
        for h in range(2):
            drain(recv_c.at[k, h, others], c_s.at[k, h])
        return 0

    lax.fori_loop(0, chunks, sent_k, 0)
    drain(recv_r.at[others], r_s)
    drain(recv_h.at[others], h_s)
    copy_e(1 - xh).wait_send()
    copy_e(xh).wait_send()
    copy_f.wait_send()
    for o in range(1, 4):
        copy_g(lax.rem(t + o, 4), t).wait_send()


def shards(final_input, norm_gain, value_weight, out_weight, cluster, priority):
    rows, width = final_input.shape
    owners = lax.axis_size("dp")
    tensor = lax.axis_size("tensor")
    part = width // tensor
    chunk = part // CHUNKS
    bucket = max(2, 2 * rows // (CLU_DEV * owners))
    side = max(16, 2 * bucket)
    per_owner = 2 * side
    capacity = owners * bucket
    kv = value_weight.shape[1]
    vmem = pl.BlockSpec(memory_space=pltpu.VMEM)
    anywhere = pl.BlockSpec(memory_space=pl.ANY)
    dma = pltpu.SemaphoreType.DMA
    best = pl.pallas_call(
        functools.partial(kernel, owners, bucket),
        out_shape=jax.ShapeDtypeStruct((1, rows), F32),
        in_specs=[anywhere, vmem, anywhere, anywhere, vmem, vmem],
        out_specs=vmem,
        scratch_shapes=[
            pltpu.VMEM((rows, width), BF16),
            pltpu.VMEM((width, kv), BF16),
            pltpu.VMEM(out_weight.shape, BF16),
            pltpu.VMEM((rows, 1), F32),
            pltpu.VMEM((rows, kv), BF16),
            pltpu.VMEM((CHUNKS, 2, rows, chunk), BF16),
            pltpu.VMEM((CHUNKS, 2, rows, chunk), BF16),
            pltpu.VMEM((CHUNKS, 2, rows, chunk), BF16),
            pltpu.VMEM((CHUNKS, rows, chunk), BF16),
            pltpu.VMEM((CHUNKS, rows, chunk), BF16),
            pltpu.VMEM((owners * per_owner, rows), BF16),
            pltpu.VMEM((CHUNKS, owners, 2, side, chunk), BF16),
            pltpu.VMEM((CHUNKS, 2, owners, side, chunk), BF16),
            pltpu.VMEM((owners, 8, 128), F32),
            pltpu.VMEM((owners, 8, 128), F32),
            pltpu.VMEM((CLU_DEV, capacity, capacity), F32),
            pltpu.VMEM((2, capacity, capacity), F32),
            pltpu.VMEM((capacity, capacity), F32),
            pltpu.VMEM((capacity, capacity), F32),
            pltpu.VMEM((CLU_DEV, 8, capacity), F32),
            pltpu.VMEM((8, 128), F32),
            pltpu.VMEM((owners, 8, 128), F32),
            dma((5,)),
            dma((CHUNKS,)), dma((CHUNKS,)),
            dma((CHUNKS,)), dma((CHUNKS,)),
            dma((CHUNKS, 2)), dma((CHUNKS, 2)),
            dma, dma,
            dma((2,)), dma((2,)),
            dma, dma,
            dma((4,)), dma((4,)),
            dma, dma,
        ],
        compiler_params=pltpu.CompilerParams(
            collective_id=0, has_side_effects=True, vmem_limit_bytes=56 * 1024 * 1024),
        cost_estimate=pl.CostEstimate(flops=6_000_000_000, bytes_accessed=16_000_000, transcendentals=0),
    )(final_input, norm_gain, value_weight, out_weight, cluster.reshape(1, rows), priority.reshape(1, rows))
    return best.reshape(rows)


def solution(mesh):
    in_specs = (P("dp", None), P(), P(None, "tensor"), P("tensor", None), P("dp", None), P("dp"))
    out_specs = P("dp")
    return jax.shard_map(shards, mesh=mesh, in_specs=in_specs, out_specs=out_specs, check_vma=False)
```
